512 devices in a mesh: ij: 4 (over x), cd: 128 (over y, z, core).
Axes of the slice: x: 4, y: 8, z: 8, core: 2. Of those that a mesh axis runs over, the one named last changes fastest.
Arguments:
- amplitudes: bfloat16 [131072, 1024], P('cd', 'ij'), may hold values from -6 to 6
- owned_columns: int32 [128, 2048], replicated, may hold values from -1 to 131071, as said below
- ladder_ints: bfloat16 [1024, 262144], P('ij', 'cd'), may hold values from -0.0625 to 0.0625
Outputs:
- ladder: bfloat16 [1024, 1024], P(('ij', 'cd'))
The draws below stay inside these ranges and needn't reach their ends.
Inputs may be any that keep to these rules, and one draw needn't show every extreme that they name: `owned_columns`: row k lists in increasing order the packed cd columns whose integrals device k of cd holds, followed by -1 in its unused slots; every column stands in exactly one row. Of each range of 1024 consecutive columns at most 16 stand in one row; some rows take exactly 16 from every range and so fill all 2048 slots.
All inputs are finite; a program needn't handle non-finite values.
Results may differ from the reference program's by a relative error of at most 0.0023.
Values may be sent and summed in bfloat16 or wider, within the bound.
No kernel may reach another device: no remote copies, remote signals or barrier semaphores. Data moves between devices by JAX's collectives and lax.ppermute only.
A program may use at most 64 MiB of HBM per device.

```python
import jax
import jax.numpy as jnp

AB = 1024
SC = 1024
IJ = 1024
NCD = 131072
MAXC = 2048
SLOTS = 262144
N_CD = 128


def owner_layout(seed_key):
    devices_cd = N_CD
    per_pair = SC // devices_cd
    heavy_count = devices_cd // 4
    light_total = devices_cd - heavy_count
    key_heavy, key_light, key_shuffle = jax.random.split(seed_key, 3)
    dest_order = jax.random.permutation(key_heavy, devices_cd).astype(jnp.int32)
    light_keys = jax.random.split(key_light, devices_cd)
    light_picks = jax.vmap(lambda one_key: jax.random.permutation(one_key, light_total))(light_keys)
    light_counts = jnp.where(light_picks < heavy_count, per_pair, per_pair // 2).astype(jnp.int32)
    counts = jnp.zeros((devices_cd, devices_cd), jnp.int32)
    counts = counts.at[:, dest_order[:heavy_count]].set(2 * per_pair)
    counts = counts.at[:, dest_order[heavy_count:]].set(light_counts)
    bounds_end = jnp.cumsum(counts, axis=1)
    positions = jnp.arange(SC, dtype=jnp.int32)
    owner_sorted = jnp.sum((bounds_end[:, None, :] <= positions[None, :, None]).astype(jnp.int32), axis=2)
    shuffle_keys = jax.random.split(key_shuffle, devices_cd)
    owners = jax.vmap(lambda one_key, row: jax.random.permutation(one_key, row))(shuffle_keys, owner_sorted)
    owners = owners.reshape(-1).astype(jnp.int32)
    grouped = jnp.argsort(owners, stable=True).astype(jnp.int32)
    totals = jnp.sum(counts, axis=0)
    starts = jnp.cumsum(totals) - totals
    dest_of = owners[grouped]
    slot_of = jnp.arange(NCD, dtype=jnp.int32) - starts[dest_of]
    owned = jnp.full((devices_cd, MAXC), -1, jnp.int32).at[dest_of, slot_of].set(grouped)
    return owned


def draw_owned_columns(key, part):
    owned = owner_layout(key)
    return owned


def spiked(drawn, own_key, source, target, shards_of, factor):
    owner, partner = [(jnp.arange(drawn.shape[position]) // (drawn.shape[position] // shards_of)).reshape([-1 if axis == position else 1 for axis in range(drawn.ndim)]) for position in (source, target)]
    chosen = jax.random.permutation(own_key, shards_of)[partner]
    strong = (owner == chosen) | (owner == (partner + shards_of // 2) % shards_of)
    return jnp.where(strong, factor * drawn, drawn)


def steps_of(stream_key, dims, cuts, low, top_value):
    def one(position, blocks):
        draws = jax.random.uniform(jax.random.fold_in(jax.random.fold_in(stream_key, 6), position), (blocks,), jnp.float32, low / len(cuts), top_value / len(cuts))
        return jnp.repeat(jnp.exp(draws), dims[position] // blocks).reshape((-1,) + (1,) * (len(dims) - position - 1))

    loudness = one(*cuts[0])
    for cut in cuts[1:]:
        loudness = loudness * one(*cut)
    return loudness


def scatter_about(stream_key, shape, scale, bound, pieces=(), kind=jnp.bfloat16):
    entries = jax.random.normal(stream_key, shape, jnp.float32) * scale
    if len(pieces) > 0:
        entries = steps_of(stream_key, shape, pieces, -0.22, 0.18) * entries
    return jnp.clip(entries, min=-bound, max=bound).astype(kind)


def heavy_noise(stream_key, dims, deviation, limit, shards, heavy, kind=jnp.bfloat16):
    entries = deviation * jax.random.normal(stream_key, dims, jnp.float32)
    if shards:
        entries = entries * steps_of(stream_key, dims, shards, -0.22, 0.18)
    return jnp.clip(spiked(entries, jax.random.fold_in(stream_key, 3), *heavy), -limit, limit).astype(kind)


def setup_inputs(seed: int = 0) -> dict:
    streams_of = jax.random.split(jax.random.key(seed), 4)
    amplitudes = scatter_about(streams_of[0], (NCD, IJ), 1.0, 6.0, ((0, 128), (1, 4)))
    owned_columns = draw_owned_columns(jax.random.fold_in(streams_of[3], 71), 0)
    ladder_ints = heavy_noise(streams_of[2], (AB, SLOTS), NCD ** -0.5, 0.0625, ((0, 4), (1, 128)), (1, 0, 128, 5.5))
    return {"amplitudes": amplitudes, "owned_columns": owned_columns, "ladder_ints": ladder_ints}


def reference(amplitudes, owned_columns, ladder_ints):
    owned_ids = owned_columns.reshape(-1)
    target = jnp.where(owned_ids >= 0, owned_ids, NCD).astype(jnp.int32)
    packed = jnp.zeros((AB, NCD + 1), ladder_ints.dtype).at[:, target].set(ladder_ints)[:, :NCD]
    return jnp.dot(packed, amplitudes, preferred_element_type=jnp.float32).astype(jnp.bfloat16)
```

```python
import jax
import jax.numpy as jnp
from jax import lax
from jax.experimental import pallas as pl
from jax.experimental.pallas import tpu as pltpu
from jax.sharding import PartitionSpec as P

F32 = jnp.float32
BF16 = jnp.bfloat16
NT = (((1,), (1,)), ((), ()))
VMEM_LIMIT = 48 * 1024 * 1024


def vmem_spec():
    return pl.BlockSpec(memory_space=pltpu.VMEM)


def identity(size):
    rows = lax.broadcasted_iota(jnp.int32, (size, size), 0)
    cols = lax.broadcasted_iota(jnp.int32, (size, size), 1)
    return jnp.where(rows == cols, 1.0, 0.0).astype(BF16)


def pack_kernel(starts, ints, out, slots):
    capacity = out.shape[1]
    total, chunk = ints.shape[1], 256
    eye = identity(chunk)
    for step in range(total // chunk):
        at = pl.ds(step * chunk, chunk)
        slots[at, :] = lax.dot_general(eye, ints[:, at], NT, preferred_element_type=F32)
    slots[pl.ds(total, capacity + 8), :] = jnp.zeros((capacity + 8, slots.shape[1]), F32)
    for dest in range(out.shape[0]):
        start = starts[dest]
        aligned = pl.multiple_of((start // 8) * 8, 8)
        window = slots[pl.ds(aligned, capacity + 8), :]
        window = pltpu.roll(window, capacity + 8 - (start - aligned), 0)
        out[dest] = window[:capacity].astype(BF16)


def order_kernel(capacity, base_ref, owned, amps, out, offsets):
    base = base_ref[0]
    holders, total = owned.shape
    width = amps.shape[0]
    beyond = jnp.int32(1 << 30)
    table = owned[...]
    table = jnp.where(table < 0, beyond, table - base)
    below = jnp.zeros((holders, 128), F32)
    ended = jnp.zeros((holders, 128), F32)
    for tile in range(total // 128):
        part = table[:, tile * 128:(tile + 1) * 128]
        below = below + jnp.where(part < 0, 1.0, 0.0)
        ended = ended + jnp.where(part < width, 1.0, 0.0)
    ones = jnp.ones((128, 128), BF16)
    below = jnp.dot(below.astype(BF16), ones, preferred_element_type=F32)
    ended = jnp.dot(ended.astype(BF16), ones, preferred_element_type=F32)
    counts = (ended - below).astype(BF16)
    rows = lax.broadcasted_iota(jnp.int32, (holders, holders), 0)
    cols = lax.broadcasted_iota(jnp.int32, (holders, holders), 1)
    earlier = jnp.where(cols < rows, 1.0, 0.0).astype(BF16)
    first = jnp.dot(earlier, counts, preferred_element_type=F32).astype(jnp.int32)
    offsets[...] = first
    start = below.astype(jnp.int32)
    window = jnp.concatenate([table, jnp.full((holders, 128), beyond, jnp.int32)], axis=1)
    shift = total // 2
    while shift >= 128:
        keep = shift + 128
        taken = (start & shift) != 0
        taken = jnp.concatenate([taken[:, :128]] * (keep // 128), axis=1)
        window = jnp.where(taken, window[:, shift:shift + keep], window[:, :keep])
        shift //= 2
    while shift >= 1:
        taken = (start & shift) != 0
        taken = jnp.concatenate([taken, taken], axis=1)
        window = jnp.where(taken, pltpu.roll(window, 256 - shift, 1), window)
        shift //= 2
    column = lax.broadcasted_iota(jnp.int32, (holders, width), 1)
    place = jnp.zeros((holders, width), jnp.int32)
    for slot in range(capacity):
        here = window[:, slot:slot + 1] == column
        place = place + jnp.where(here, first[:, :1] + slot, 0)
    place = jnp.sum(place, axis=0, keepdims=True)
    chunk = 256
    values = amps[...]
    for step in range(width // chunk):
        wanted = lax.broadcasted_iota(jnp.int32, (chunk, width), 0) + step * chunk
        pick = jnp.where(wanted == place, 1.0, 0.0).astype(BF16)
        out[pl.ds(step * chunk, chunk), :] = jnp.dot(
            pick, values, preferred_element_type=F32
        ).astype(BF16)


def multiply_kernel(offsets, where_ref, received, amps0, amps1, amps2, amps3, kept, given, rows_ref, result):
    group, core = where_ref[0], where_ref[1]
    holders, capacity, pairs = received.shape
    width = amps0.shape[0]
    line = lax.broadcasted_iota(jnp.int32, (capacity + 8, pairs), 0)
    blank = jnp.zeros((8, pairs), F32)
    for holder in range(holders):
        start = offsets[holder]
        aligned = pl.multiple_of((start // 8) * 8, 8)
        at = pl.ds(aligned, capacity + 8)
        window = jnp.concatenate([received[holder].astype(F32), blank], axis=0)
        window = pltpu.roll(window, start - aligned, 0)
        rows_ref[at, :] = jnp.where(line < start - aligned, rows_ref[at, :], window)
    new = lax.broadcasted_iota(jnp.int32, (pairs, pairs), 0)
    old = lax.broadcasted_iota(jnp.int32, (pairs, pairs), 1)
    half = pairs // 2
    chips = half // 2
    side = jnp.where(new < half, core, 1 - core)
    in_half = jnp.where(new < half, new, new - half)
    row = jnp.where(in_half < chips, 0, 1)
    chip = jnp.where(in_half < chips, in_half, in_half - chips)
    pick = jnp.where(old == 4 * chip + 2 * side + row, 1.0, 0.0).astype(BF16)
    left = jnp.concatenate(
        [
            lax.dot_general(
                pick,
                rows_ref[pl.ds(step * 256, 256), :].astype(BF16),
                NT,
                preferred_element_type=F32,
            ).astype(BF16)
            for step in range(width // 256)
        ],
        axis=1,
    )
    for step, amps in enumerate((amps0, amps1, amps2, amps3)):
        block = lax.rem(group + step, 4)
        product = jnp.dot(left, amps[...], preferred_element_type=F32)
        result[:, pl.ds(pl.multiple_of(block * 256, 256), 256)] = product
    for target, at in ((kept, 0), (given, half)):
        for r in range(2):
            for j in range(8):
                target[pl.ds(r * 8 + j, chips, stride=16), :] = result[
                    at + r * chips:at + (r + 1) * chips, j * 128:(j + 1) * 128
                ]


def body(amplitudes, owned_columns, ladder_ints):
    device = lax.axis_index("cd")
    group = lax.axis_index("ij")
    devices_cd = lax.axis_size("cd")
    width, pairs_ij = amplitudes.shape
    pairs_ab, slot_total = ladder_ints.shape
    capacity = 2 * width // devices_cd
    base = device * width
    params = pltpu.CompilerParams(vmem_limit_bytes=VMEM_LIMIT)
    smem = pl.BlockSpec(memory_space=pltpu.SMEM)

    own_row = lax.dynamic_index_in_dim(owned_columns, device, 0, keepdims=False)
    range_starts = jnp.arange(devices_cd, dtype=jnp.int32) * width
    starts = jnp.sum(
        (own_row >= 0)[None, :] & (own_row[None, :] < range_starts[:, None]), axis=1, dtype=jnp.int32
    )
    outgoing = pl.pallas_call(
        pack_kernel,
        out_shape=jax.ShapeDtypeStruct((devices_cd, capacity, pairs_ab), BF16),
        in_specs=[smem, vmem_spec()],
        out_specs=vmem_spec(),
        scratch_shapes=[pltpu.VMEM((slot_total + capacity + 8, pairs_ab), F32)],
        compiler_params=params,
        name="pack",
    )(starts, ladder_ints)
    incoming = lax.all_to_all(outgoing, "cd", split_axis=0, concat_axis=0, tiled=True)

    ordered, offsets = pl.pallas_call(
        lambda *refs: order_kernel(capacity, *refs),
        out_shape=[
            jax.ShapeDtypeStruct((width, pairs_ij), BF16),
            jax.ShapeDtypeStruct((devices_cd, 128), jnp.int32),
        ],
        in_specs=[smem, vmem_spec(), vmem_spec()],
        out_specs=[vmem_spec(), vmem_spec()],
        compiler_params=params,
        name="order",
    )(base[None].astype(jnp.int32), owned_columns, amplitudes)
    groups = lax.axis_size("ij")
    others = [
        lax.ppermute(ordered, "ij", [((i + step) % groups, i) for i in range(groups)])
        for step in range(1, groups)
    ]
    core = lax.rem(device, 2)
    half = pairs_ab // 2
    kept, given = pl.pallas_call(
        multiply_kernel,
        out_shape=[jax.ShapeDtypeStruct((8 * pairs_ab // 2 // 2 * 2, 128), F32)] * 2,
        in_specs=[smem, smem] + [vmem_spec()] * 5,
        out_specs=[vmem_spec(), vmem_spec()],
        scratch_shapes=[
            pltpu.VMEM((width + capacity + 8, pairs_ab), F32),
            pltpu.VMEM((pairs_ab, groups * pairs_ij), F32),
        ],
        compiler_params=params,
        name="multiply",
    )(offsets[:, 0], jnp.stack([group, core]).astype(jnp.int32), incoming, ordered, *others)
    taken = lax.ppermute(given, "cd", [(i, i ^ 1) for i in range(devices_cd)])
    both = (kept + taken).reshape(devices_cd // 2, 16, 128)
    same_core = [[2 * k + c for k in range(devices_cd // 2)] for c in range(2)]
    shares = lax.all_to_all(both, "cd", 0, 0, tiled=True, axis_index_groups=same_core)
    summed = jnp.sum(shares, axis=0)
    return summed.astype(BF16).reshape(2, 1024)


def solution(mesh):
    return jax.shard_map(
        body,
        mesh=mesh,
        in_specs=(P("cd", "ij"), P(), P("ij", "cd")),
        out_specs=P(("ij", "cd"), None),
        check_vma=False,
    )
```

```python
import jax
import jax.numpy as jnp
from jax import lax
from jax.experimental import pallas as pl
from jax.experimental.pallas import tpu as pltpu
from jax.sharding import PartitionSpec as P

F32 = jnp.float32
BF16 = jnp.bfloat16
NT = (((1,), (1,)), ((), ()))
VMEM_LIMIT = 48 * 1024 * 1024


def vmem_spec():
    return pl.BlockSpec(memory_space=pltpu.VMEM)


def identity(size):
    rows = lax.broadcasted_iota(jnp.int32, (size, size), 0)
    cols = lax.broadcasted_iota(jnp.int32, (size, size), 1)
    return jnp.where(rows == cols, 1.0, 0.0).astype(BF16)


def pack_kernel(starts, ints, out, slots):
    capacity = out.shape[1]
    total, chunk = ints.shape[1], 256
    eye = identity(chunk)
    for step in range(total // chunk):
        at = pl.ds(step * chunk, chunk)
        slots[at, :] = lax.dot_general(eye, ints[:, at], NT, preferred_element_type=F32)
    slots[pl.ds(total, capacity + 8), :] = jnp.zeros((capacity + 8, slots.shape[1]), F32)
    for dest in range(out.shape[0]):
        start = starts[dest]
        aligned = pl.multiple_of((start // 8) * 8, 8)
        window = slots[pl.ds(aligned, capacity + 8), :]
        window = pltpu.roll(window, capacity + 8 - (start - aligned), 0)
        out[dest] = window[:capacity].astype(BF16)


def order_kernel(capacity, base_ref, owned, out):
    base = base_ref[0]
    holders, total = owned.shape
    width = out.shape[0]
    beyond = jnp.int32(1 << 30)
    table = owned[...]
    table = jnp.where(table < 0, beyond, table - base)
    below = jnp.zeros((holders, 128), F32)
    for tile in range(total // 128):
        below = below + jnp.where(table[:, tile * 128:(tile + 1) * 128] < 0, 1.0, 0.0)
    ones = jnp.ones((128, 128), BF16)
    start = jnp.dot(below.astype(BF16), ones, preferred_element_type=F32).astype(jnp.int32)
    window = jnp.concatenate([table, jnp.full((holders, 128), beyond, jnp.int32)], axis=1)
    shift = total // 2
    while shift >= 128:
        keep = shift + 128
        taken = (start & shift) != 0
        taken = jnp.concatenate([taken] * (keep // 128), axis=1)
        window = jnp.where(taken, window[:, shift:shift + keep], window[:, :keep])
        shift //= 2
    while shift >= 1:
        taken = (start & shift) != 0
        taken = jnp.concatenate([taken, taken], axis=1)
        window = jnp.where(taken, pltpu.roll(window, 256 - shift, 1), window)
        shift //= 2
    lane = lax.broadcasted_iota(jnp.int32, (holders, 128), 1)
    spread = jnp.where(lane < capacity, window[:, :128], 0)
    shift = capacity
    while shift < 128:
        spread = spread + pltpu.roll(spread, shift, 1)
        shift *= 2
    each = 128 // capacity
    mine = lax.broadcasted_iota(jnp.int32, (each, 128), 0)
    mine = mine == lax.broadcasted_iota(jnp.int32, (each, 128), 1) // capacity
    columns = jnp.concatenate(
        [
            jnp.sum(jnp.where(mine, spread[at:at + each], 0), axis=0, keepdims=True)
            for at in range(0, holders, each)
        ],
        axis=1,
    )
    chunk = 128
    for step in range(width // chunk):
        wanted = lax.broadcasted_iota(jnp.int32, (chunk, holders * capacity), 0) + step * chunk
        out[pl.ds(step * chunk, chunk), :] = jnp.where(wanted == columns, 1.0, 0.0).astype(BF16)


def multiply_kernel(where_ref, received, order, amps0, amps1, amps2, amps3, kept, given, result):
    group, core = where_ref[0], where_ref[1]
    holders, capacity, pairs = received.shape
    new = lax.broadcasted_iota(jnp.int32, (pairs, pairs), 0)
    old = lax.broadcasted_iota(jnp.int32, (pairs, pairs), 1)
    half = pairs // 2
    chips = half // 2
    side = jnp.where(new < half, core, 1 - core)
    in_half = jnp.where(new < half, new, new - half)
    row = jnp.where(in_half < chips, 0, 1)
    chip = jnp.where(in_half < chips, in_half, in_half - chips)
    pick = jnp.where(old == 4 * chip + 2 * side + row, 1.0, 0.0).astype(BF16)
    columns = received[...].reshape(holders * capacity, pairs)
    slots = lax.dot_general(pick, columns, NT, preferred_element_type=F32).astype(BF16)
    left = lax.dot_general(slots, order[...], NT, preferred_element_type=F32).astype(BF16)
    for step, amps in enumerate((amps0, amps1, amps2, amps3)):
        block = lax.rem(group + step, 4)
        product = jnp.dot(left, amps[...], preferred_element_type=F32)
        result[:, pl.ds(pl.multiple_of(block * 256, 256), 256)] = product
    for target, at in ((kept, 0), (given, half)):
        for r in range(2):
            for j in range(8):
                target[pl.ds(r * 8 + j, chips, stride=16), :] = result[
                    at + r * chips:at + (r + 1) * chips, j * 128:(j + 1) * 128
                ]


def body(amplitudes, owned_columns, ladder_ints):
    device = lax.axis_index("cd")
    group = lax.axis_index("ij")
    devices_cd = lax.axis_size("cd")
    width, pairs_ij = amplitudes.shape
    pairs_ab, slot_total = ladder_ints.shape
    capacity = 2 * width // devices_cd
    base = device * width
    params = pltpu.CompilerParams(vmem_limit_bytes=VMEM_LIMIT)
    smem = pl.BlockSpec(memory_space=pltpu.SMEM)

    own_row = lax.dynamic_index_in_dim(owned_columns, device, 0, keepdims=False)
    range_starts = jnp.arange(devices_cd, dtype=jnp.int32) * width
    starts = jnp.sum(
        (own_row >= 0)[None, :] & (own_row[None, :] < range_starts[:, None]), axis=1, dtype=jnp.int32
    )
    outgoing = pl.pallas_call(
        pack_kernel,
        out_shape=jax.ShapeDtypeStruct((devices_cd, capacity, pairs_ab), BF16),
        in_specs=[smem, vmem_spec()],
        out_specs=vmem_spec(),
        scratch_shapes=[pltpu.VMEM((slot_total + capacity + 8, pairs_ab), F32)],
        compiler_params=params,
        name="pack",
    )(starts, ladder_ints)
    incoming = lax.all_to_all(outgoing, "cd", split_axis=0, concat_axis=0, tiled=True)

    order = pl.pallas_call(
        lambda *refs: order_kernel(capacity, *refs),
        out_shape=jax.ShapeDtypeStruct((width, devices_cd * capacity), BF16),
        in_specs=[smem, vmem_spec()],
        out_specs=vmem_spec(),
        compiler_params=params,
        name="order",
    )(base[None].astype(jnp.int32), owned_columns)
    groups = lax.axis_size("ij")
    others = [
        lax.ppermute(amplitudes, "ij", [((i + step) % groups, i) for i in range(groups)])
        for step in range(1, groups)
    ]
    core = lax.rem(device, 2)
    half = pairs_ab // 2
    kept, given = pl.pallas_call(
        multiply_kernel,
        out_shape=[jax.ShapeDtypeStruct((half * groups * pairs_ij // 128, 128), F32)] * 2,
        in_specs=[smem] + [vmem_spec()] * 6,
        out_specs=[vmem_spec(), vmem_spec()],
        scratch_shapes=[pltpu.VMEM((pairs_ab, groups * pairs_ij), F32)],
        compiler_params=params,
        name="multiply",
    )(jnp.stack([group, core]).astype(jnp.int32), incoming, order, amplitudes, *others)
    taken = lax.ppermute(given, "cd", [(i, i ^ 1) for i in range(devices_cd)])
    both = (kept + taken).reshape(devices_cd // 2, 16, 128)
    same_core = [[2 * k + c for k in range(devices_cd // 2)] for c in range(2)]
    shares = lax.all_to_all(both, "cd", 0, 0, tiled=True, axis_index_groups=same_core)
    summed = jnp.sum(shares, axis=0)
    return summed.astype(BF16).reshape(2, 1024)


def solution(mesh):
    return jax.shard_map(
        body,
        mesh=mesh,
        in_specs=(P("cd", "ij"), P(), P("ij", "cd")),
        out_specs=P(("ij", "cd"), None),
        check_vma=False,
    )
```

```python
import jax
import jax.numpy as jnp
from jax import lax
from jax.experimental import pallas as pl
from jax.experimental.pallas import tpu as pltpu
from jax.sharding import PartitionSpec as P

F32 = jnp.float32
BF16 = jnp.bfloat16
NT = (((1,), (1,)), ((), ()))
VMEM_LIMIT = 24 * 1024 * 1024


def vmem_spec():
    return pl.BlockSpec(memory_space=pltpu.VMEM)


def identity(size):
    rows = lax.broadcasted_iota(jnp.int32, (size, size), 0)
    cols = lax.broadcasted_iota(jnp.int32, (size, size), 1)
    return jnp.where(rows == cols, 1.0, 0.0).astype(BF16)


def pack_kernel(where_ref, owned, ints, out, group, staged, slots, firsts, starts, sems):
    device = where_ref[0]
    devices, capacity, _ = out.shape
    total, chunk = ints.shape[1], 256
    steps = total // chunk
    eight = pl.multiple_of((device // 8) * 8, 8)
    own_copy = pltpu.make_async_copy(owned.at[pl.ds(eight, 8)], group, sems.at[steps])
    own_copy.start()
    copies = []
    for step in range(steps):
        at = pl.ds(step * chunk, chunk)
        copies.append(pltpu.make_async_copy(ints.at[:, at], staged.at[:, at], sems.at[step]))
        copies[-1].start()
    slots[pl.ds(total, capacity + 8), :] = jnp.zeros((capacity + 8, slots.shape[1]), F32)
    own_copy.wait()
    line = lax.broadcasted_iota(jnp.int32, group.shape, 0)
    row = jnp.sum(jnp.where(line == device - eight, group[...], 0), axis=0, keepdims=True)
    row = jnp.where(row < 0, jnp.int32(1 << 30), row)
    width = lax.broadcasted_iota(jnp.int32, (devices, 128), 0) * where_ref[1]
    before = jnp.zeros((devices, 128), F32)
    for tile in range(total // 128):
        before = before + jnp.where(row[:, tile * 128:(tile + 1) * 128] < width, 1.0, 0.0)
    ones = jnp.ones((128, 128), BF16)
    before = jnp.dot(before.astype(BF16), ones, preferred_element_type=F32)
    same = lax.broadcasted_iota(jnp.int32, (devices, 128), 0) == lax.broadcasted_iota(
        jnp.int32, (devices, 128), 1
    )
    first = jnp.sum(jnp.where(same, before, 0.0), axis=0, keepdims=True).astype(jnp.int32)
    firsts[...] = jnp.broadcast_to(first, firsts.shape)
    out_copy = pltpu.make_async_copy(firsts, starts, sems.at[steps + 1])
    out_copy.start()
    eye = identity(chunk)
    for step in range(steps):
        at = pl.ds(step * chunk, chunk)
        copies[step].wait()
        slots[at, :] = lax.dot_general(eye, staged[:, at], NT, preferred_element_type=F32)
    out_copy.wait()
    for dest in range(devices):
        start = starts[0, dest]
        aligned = pl.multiple_of((start // 8) * 8, 8)
        window = slots[pl.ds(aligned, capacity + 8), :]
        window = pltpu.roll(window, capacity + 8 - (start - aligned), 0)
        out[dest] = window[:capacity].astype(BF16)


def order_kernel(capacity, base_ref, owned, out):
    base = base_ref[0]
    holders, total = owned.shape
    width = out.shape[0]
    beyond = jnp.int32(1 << 30)
    table = owned[...]
    table = jnp.where(table < 0, beyond, table - base)
    below = jnp.zeros((holders, 128), F32)
    for tile in range(total // 128):
        below = below + jnp.where(table[:, tile * 128:(tile + 1) * 128] < 0, 1.0, 0.0)
    ones = jnp.ones((128, 128), BF16)
    start = jnp.dot(below.astype(BF16), ones, preferred_element_type=F32).astype(jnp.int32)
    window = jnp.concatenate([table, jnp.full((holders, 128), beyond, jnp.int32)], axis=1)
    shift = total // 2
    while shift >= 128:
        keep = shift + 128
        taken = (start & shift) != 0
        taken = jnp.concatenate([taken] * (keep // 128), axis=1)
        window = jnp.where(taken, window[:, shift:shift + keep], window[:, :keep])
        shift //= 2
    while shift >= 1:
        taken = (start & shift) != 0
        taken = jnp.concatenate([taken, taken], axis=1)
        window = jnp.where(taken, pltpu.roll(window, 256 - shift, 1), window)
        shift //= 2
    lane = lax.broadcasted_iota(jnp.int32, (holders, 128), 1)
    spread = jnp.where(lane < capacity, window[:, :128], 0)
    shift = capacity
    while shift < 128:
        spread = spread + pltpu.roll(spread, shift, 1)
        shift *= 2
    each = 128 // capacity
    mine = lax.broadcasted_iota(jnp.int32, (each, 128), 0)
    mine = mine == lax.broadcasted_iota(jnp.int32, (each, 128), 1) // capacity
    columns = jnp.concatenate(
        [
            jnp.sum(jnp.where(mine, spread[at:at + each], 0), axis=0, keepdims=True)
            for at in range(0, holders, each)
        ],
        axis=1,
    )
    chunk = 128
    for step in range(width // chunk):
        wanted = lax.broadcasted_iota(jnp.int32, (chunk, holders * capacity), 0) + step * chunk
        out[pl.ds(step * chunk, chunk), :] = jnp.where(wanted == columns, 1.0, 0.0).astype(BF16)


def multiply_kernel(where_ref, received, order, amps0, amps1, amps2, amps3, kept, given, result):
    group, core = where_ref[0], where_ref[1]
    holders, capacity, pairs = received.shape
    new = lax.broadcasted_iota(jnp.int32, (pairs, pairs), 0)
    old = lax.broadcasted_iota(jnp.int32, (pairs, pairs), 1)
    half = pairs // 2
    chips = half // 2
    side = jnp.where(new < half, core, 1 - core)
    in_half = jnp.where(new < half, new, new - half)
    row = jnp.where(in_half < chips, 0, 1)
    chip = jnp.where(in_half < chips, in_half, in_half - chips)
    pick = jnp.where(old == 4 * chip + 2 * side + row, 1.0, 0.0).astype(BF16)
    columns = received[...].reshape(holders * capacity, pairs)
    slots = lax.dot_general(pick, columns, NT, preferred_element_type=F32).astype(BF16)
    left = lax.dot_general(slots, order[...], NT, preferred_element_type=F32).astype(BF16)
    for step, amps in enumerate((amps0, amps1, amps2, amps3)):
        block = lax.rem(group + step, 4)
        product = jnp.dot(left, amps[...], preferred_element_type=F32)
        result[:, pl.ds(pl.multiple_of(block * 256, 256), 256)] = product
    for target, at in ((kept, 0), (given, half)):
        for r in range(2):
            for j in range(8):
                target[pl.ds(r * 8 + j, chips, stride=16), :] = result[
                    at + r * chips:at + (r + 1) * chips, j * 128:(j + 1) * 128
                ]


SCALE = 2.0 ** 22


def squeeze(value):
    return (jnp.sign(value) * jnp.sqrt(jnp.abs(value) * SCALE)).astype(jnp.float16)


def unsqueeze(root):
    root = root.astype(F32)
    return root * jnp.abs(root) * (1.0 / SCALE)


def body(amplitudes, owned_columns, ladder_ints):
    device = lax.axis_index("cd")
    group = lax.axis_index("ij")
    devices_cd = lax.axis_size("cd")
    width, pairs_ij = amplitudes.shape
    pairs_ab, slot_total = ladder_ints.shape
    capacity = 2 * width // devices_cd
    base = device * width
    params = pltpu.CompilerParams(vmem_limit_bytes=VMEM_LIMIT)
    smem = pl.BlockSpec(memory_space=pltpu.SMEM)

    outgoing = pl.pallas_call(
        pack_kernel,
        out_shape=jax.ShapeDtypeStruct((devices_cd, capacity, pairs_ab), BF16),
        in_specs=[smem] + [pl.BlockSpec(memory_space=pltpu.HBM)] * 2,
        out_specs=vmem_spec(),
        scratch_shapes=[
            pltpu.VMEM((8, slot_total), jnp.int32),
            pltpu.VMEM((pairs_ab, slot_total), BF16),
            pltpu.VMEM((slot_total + capacity + 8, pairs_ab), F32),
            pltpu.VMEM((8, 128), jnp.int32),
            pltpu.SMEM((8, 128), jnp.int32),
            pltpu.SemaphoreType.DMA((slot_total // 256 + 2,)),
        ],
        compiler_params=params,
        name="pack",
    )(jnp.stack([device, jnp.int32(width)]).astype(jnp.int32), owned_columns, ladder_ints)
    incoming = lax.all_to_all(outgoing, "cd", split_axis=0, concat_axis=0, tiled=True)

    order = pl.pallas_call(
        lambda *refs: order_kernel(capacity, *refs),
        out_shape=jax.ShapeDtypeStruct((width, devices_cd * capacity), BF16),
        in_specs=[smem, vmem_spec()],
        out_specs=vmem_spec(),
        compiler_params=params,
        name="order",
    )(base[None].astype(jnp.int32), owned_columns)
    groups = lax.axis_size("ij")
    others = [
        lax.ppermute(amplitudes, "ij", [((i + step) % groups, i) for i in range(groups)])
        for step in range(1, groups)
    ]
    core = lax.rem(device, 2)
    half = pairs_ab // 2
    kept, given = pl.pallas_call(
        multiply_kernel,
        out_shape=[jax.ShapeDtypeStruct((half * groups * pairs_ij // 128, 128), F32)] * 2,
        in_specs=[smem] + [vmem_spec()] * 6,
        out_specs=[vmem_spec(), vmem_spec()],
        scratch_shapes=[pltpu.VMEM((pairs_ab, groups * pairs_ij), F32)],
        compiler_params=params,
        name="multiply",
    )(jnp.stack([group, core]).astype(jnp.int32), incoming, order, amplitudes, *others)
    taken = lax.ppermute(given, "cd", [(i, i ^ 1) for i in range(devices_cd)])
    both = squeeze(kept + taken).reshape(devices_cd // 2, 16, 128)
    same_core = [[2 * k + c for k in range(devices_cd // 2)] for c in range(2)]
    shares = lax.all_to_all(both, "cd", 0, 0, tiled=True, axis_index_groups=same_core)
    summed = jnp.sum(unsqueeze(shares), axis=0)
    return summed.astype(BF16).reshape(2, 1024)


def solution(mesh):
    return jax.shard_map(
        body,
        mesh=mesh,
        in_specs=(P("cd", "ij"), P(), P("ij", "cd")),
        out_specs=P(("ij", "cd"), None),
        check_vma=False,
    )
```

```python
import jax
import jax.numpy as jnp
from jax import lax
from jax.experimental import pallas as pl
from jax.experimental.pallas import tpu as pltpu
from jax.sharding import PartitionSpec as P

F32 = jnp.float32
BF16 = jnp.bfloat16
NT = (((1,), (1,)), ((), ()))
VMEM_LIMIT = 24 * 1024 * 1024
VMEM = pl.BlockSpec(memory_space=pltpu.VMEM)
SMEM = pl.BlockSpec(memory_space=pltpu.SMEM)
ANY = pl.BlockSpec(memory_space=pl.ANY)
HBM = pl.BlockSpec(memory_space=pltpu.HBM)


def in_hbm(value):
    return pltpu.with_memory_space_constraint(value, pltpu.HBM)


def pack_kernel(starts, ints, out, slots, windows, sems):
    devices, capacity, _ = out.shape
    total, chunk = ints.shape[1], 256
    rows = lax.broadcasted_iota(jnp.int32, (chunk, chunk), 0)
    cols = lax.broadcasted_iota(jnp.int32, (chunk, chunk), 1)
    eye = jnp.where(rows == cols, 1.0, 0.0).astype(BF16)
    for step in range(total // chunk):
        at = pl.ds(step * chunk, chunk)
        slots[at, :] = lax.dot_general(eye, ints[:, at], NT, preferred_element_type=F32)
    slots[pl.ds(total, capacity + 8), :] = jnp.zeros((capacity + 8, slots.shape[1]), F32)
    pieces = sems.shape[0]
    each = devices // pieces
    copies = []
    for piece in range(pieces):
        for dest in range(piece * each, (piece + 1) * each):
            start = starts[dest]
            aligned = pl.multiple_of((start >> 3) << 3, 8)
            window = slots[pl.ds(aligned, capacity + 8), :]
            window = pltpu.roll(window, capacity + 8 - (start & 7), 0)
            windows[dest] = window[:capacity].astype(BF16)
        at = pl.ds(piece * each, each)
        copies.append(pltpu.make_async_copy(windows.at[at], out.at[at], sems.at[piece]))
        copies[-1].start()
    for copy in copies:
        copy.wait()


def order_kernel(capacity, width, base_ref, owned, out, held, sem):
    copy = pltpu.make_async_copy(owned, held, sem)
    copy.start()
    base = base_ref[0]
    holders, total = owned.shape
    beyond = jnp.int32(1 << 30)
    copy.wait()
    table = held[...]
    table = jnp.where(table < 0, beyond, table - base)
    below = jnp.zeros((holders, 128), F32)
    for tile in range(total // 128):
        below = below + jnp.where(table[:, tile * 128:(tile + 1) * 128] < 0, 1.0, 0.0)
    ones = jnp.ones((128, 128), BF16)
    start = jnp.dot(below.astype(BF16), ones, preferred_element_type=F32).astype(jnp.int32)
    window = jnp.concatenate([table, jnp.full((holders, 128), beyond, jnp.int32)], axis=1)
    shift = total // 2
    while shift >= 128:
        keep = shift + 128
        taken = (start & shift) != 0
        taken = jnp.concatenate([taken] * (keep // 128), axis=1)
        window = jnp.where(taken, window[:, shift:shift + keep], window[:, :keep])
        shift //= 2
    while shift >= 1:
        taken = (start & shift) != 0
        taken = jnp.concatenate([taken, taken], axis=1)
        window = jnp.where(taken, pltpu.roll(window, 256 - shift, 1), window)
        shift //= 2
    lane = lax.broadcasted_iota(jnp.int32, (holders, 128), 1)
    spread = jnp.where(lane < capacity, window[:, :128], 0)
    shift = capacity
    while shift < 128:
        spread = spread + pltpu.roll(spread, shift, 1)
        shift *= 2
    each = 128 // capacity
    mine = lax.broadcasted_iota(jnp.int32, (each, 128), 0)
    mine = mine == lax.broadcasted_iota(jnp.int32, (each, 128), 1) // capacity
    columns = jnp.concatenate(
        [
            jnp.sum(jnp.where(mine, spread[at:at + each], 0), axis=0, keepdims=True)
            for at in range(0, holders, each)
        ],
        axis=1,
    )
    out[...] = jnp.broadcast_to(columns, out.shape)


def multiply_kernel(
    where_ref, received, columns, amps0, amps1, amps2, amps3, kept, given, left, amps, sems
):
    group, core = where_ref[0], where_ref[1]
    holders, capacity, pairs = received.shape
    blocks, width, _ = amps.shape
    copies = []
    for step, part in enumerate((amps0, amps1, amps2, amps3)):
        target = amps.at[lax.rem(group + step, blocks)]
        copies.append(pltpu.make_async_copy(part, target, sems.at[step]))
        copies[-1].start()
    new = lax.broadcasted_iota(jnp.int32, (pairs, pairs), 0)
    old = lax.broadcasted_iota(jnp.int32, (pairs, pairs), 1)
    half = pairs // 2
    chips = half // 2
    side = jnp.where(new < half, core, 1 - core)
    in_half = jnp.where(new < half, new, new - half)
    row = jnp.where(in_half < chips, 0, 1)
    chip = jnp.where(in_half < chips, in_half, in_half - chips)
    pick = jnp.where(old == 4 * chip + 2 * side + row, 1.0, 0.0).astype(BF16)
    slot_count = holders * capacity
    slots = lax.dot_general(
        pick, received[...].reshape(slot_count, pairs), NT, preferred_element_type=F32
    ).astype(BF16)
    place = columns[0:1, :]
    chunk = 256
    for step in range(width // chunk):
        wanted = lax.broadcasted_iota(jnp.int32, (chunk, slot_count), 0) + step * chunk
        order = jnp.where(wanted == place, 1.0, 0.0).astype(BF16)
        left[:, step * chunk:(step + 1) * chunk] = lax.dot_general(
            slots, order, NT, preferred_element_type=F32
        ).astype(BF16)
    for copy in copies:
        copy.wait()
    for block in range(blocks):
        product = jnp.dot(left[...], amps[block], preferred_element_type=F32)
        for target, at in ((kept, 0), (given, half)):
            for r in range(2):
                for h in range(2):
                    target[pl.ds(r * 8 + 2 * block + h, chips, stride=16), :] = product[
                        at + r * chips:at + (r + 1) * chips, h * 128:(h + 1) * 128
                    ]


def pack(starts, ladder_ints, devices, capacity):
    pairs, total = ladder_ints.shape
    return pl.pallas_call(
        pack_kernel,
        out_shape=jax.ShapeDtypeStruct((devices, capacity, pairs), BF16),
        in_specs=[SMEM, VMEM],
        out_specs=HBM,
        scratch_shapes=[
            pltpu.VMEM((total + capacity + 8, pairs), F32),
            pltpu.VMEM((devices, capacity, pairs), BF16),
            pltpu.SemaphoreType.DMA((8,)),
        ],
        compiler_params=pltpu.CompilerParams(vmem_limit_bytes=VMEM_LIMIT),
        name="pack",
    )(starts, ladder_ints)


def order(base, owned_columns, capacity, width):
    holders, _ = owned_columns.shape
    return pl.pallas_call(
        lambda *refs: order_kernel(capacity, width, *refs),
        out_shape=jax.ShapeDtypeStruct((8, holders * capacity), jnp.int32),
        in_specs=[SMEM, HBM],
        out_specs=VMEM,
        scratch_shapes=[
            pltpu.VMEM(owned_columns.shape, jnp.int32),
            pltpu.SemaphoreType.DMA,
        ],
        compiler_params=pltpu.CompilerParams(vmem_limit_bytes=VMEM_LIMIT),
        name="order",
    )(base, in_hbm(owned_columns))


def multiply(where, received, columns, amps0, amps1, amps2, amps3):
    pairs = received.shape[2]
    width, pairs_ij = amps0.shape
    out = jax.ShapeDtypeStruct((pairs // 2 * 4 * pairs_ij // 128, 128), F32)
    return pl.pallas_call(
        multiply_kernel,
        out_shape=[out, out],
        in_specs=[SMEM, VMEM, VMEM] + [ANY] * 4,
        out_specs=[VMEM, VMEM],
        scratch_shapes=[
            pltpu.VMEM((pairs, width), BF16),
            pltpu.VMEM((4, width, pairs_ij), BF16),
            pltpu.SemaphoreType.DMA((4,)),
        ],
        compiler_params=pltpu.CompilerParams(vmem_limit_bytes=VMEM_LIMIT),
        name="multiply",
    )(where, received, columns, amps0, amps1, amps2, amps3)


SCALE = 2.0 ** 22


def squeeze(value):
    return (jnp.sign(value) * jnp.sqrt(jnp.abs(value) * SCALE)).astype(jnp.float16)


def unsqueeze(root):
    root = root.astype(F32)
    return root * jnp.abs(root) * (1.0 / SCALE)


def body(amplitudes, owned_columns, ladder_ints):
    device = lax.axis_index("cd")
    group = lax.axis_index("ij")
    devices_cd = lax.axis_size("cd")
    groups = lax.axis_size("ij")
    width = amplitudes.shape[0]
    capacity = 2 * width // devices_cd

    own_row = lax.dynamic_index_in_dim(owned_columns, device, 0, keepdims=False)
    range_starts = jnp.arange(devices_cd, dtype=jnp.int32) * width
    starts = jnp.sum(
        (own_row >= 0)[None, :] & (own_row[None, :] < range_starts[:, None]), axis=1, dtype=jnp.int32
    )
    outgoing = pack(starts, ladder_ints, devices_cd, capacity)
    incoming = lax.all_to_all(outgoing, "cd", split_axis=0, concat_axis=0, tiled=True)
    columns = order((device * width)[None].astype(jnp.int32), owned_columns, capacity, width)

    def from_group(value, step):
        return lax.ppermute(value, "ij", [((i + step) % groups, i) for i in range(groups)])

    others = [from_group(amplitudes, step) for step in range(1, groups)]
    where = jnp.stack([group, lax.rem(device, 2)]).astype(jnp.int32)
    kept, given = multiply(where, incoming, columns, amplitudes, *others)
    taken = lax.ppermute(given, "cd", [(i, i ^ 1) for i in range(devices_cd)])
    both = squeeze(kept + taken).reshape(devices_cd // 2, 16, 128)
    same_core = [[2 * k + c for k in range(devices_cd // 2)] for c in range(2)]
    shares = lax.all_to_all(both, "cd", 0, 0, tiled=True, axis_index_groups=same_core)
    summed = jnp.sum(unsqueeze(shares), axis=0)
    return summed.astype(BF16).reshape(2, 1024)


def solution(mesh):
    return jax.shard_map(
        body,
        mesh=mesh,
        in_specs=(P("cd", "ij"), P(), P("ij", "cd")),
        out_specs=P(("ij", "cd"), None),
        check_vma=False,
    )
```

```python
import jax
import jax.numpy as jnp
from jax import lax
from jax.experimental import pallas as pl
from jax.experimental.pallas import tpu as pltpu
from jax.sharding import PartitionSpec as P

F32 = jnp.float32
BF16 = jnp.bfloat16
NT = (((1,), (1,)), ((), ()))
VMEM_LIMIT = 24 * 1024 * 1024
VMEM = pl.BlockSpec(memory_space=pltpu.VMEM)
SMEM = pl.BlockSpec(memory_space=pltpu.SMEM)
ANY = pl.BlockSpec(memory_space=pl.ANY)
HBM = pl.BlockSpec(memory_space=pltpu.HBM)


def in_hbm(value):
    return pltpu.with_memory_space_constraint(value, pltpu.HBM)


def pack_kernel(where_ref, owned, ints, out, group, staged, slots, firsts, starts, windows, sems):
    device, width = where_ref[0], where_ref[1]
    devices, capacity, _ = out.shape
    total, chunk = ints.shape[1], 256
    eight = pl.multiple_of((device >> 3) << 3, 8)
    own_copy = pltpu.make_async_copy(owned.at[pl.ds(eight, 8)], group, sems.at[0])
    own_copy.start()
    ints_copy = pltpu.make_async_copy(ints, staged, sems.at[1])
    ints_copy.start()
    slots[pl.ds(total, capacity + 8), :] = jnp.zeros((capacity + 8, slots.shape[1]), F32)
    rows = lax.broadcasted_iota(jnp.int32, (chunk, chunk), 0)
    cols = lax.broadcasted_iota(jnp.int32, (chunk, chunk), 1)
    eye = jnp.where(rows == cols, 1.0, 0.0).astype(BF16)
    line = lax.broadcasted_iota(jnp.int32, group.shape, 0)
    below = lax.broadcasted_iota(jnp.int32, (devices, 128), 0) * width
    same = lax.broadcasted_iota(jnp.int32, (devices, 128), 0) == lax.broadcasted_iota(
        jnp.int32, (devices, 128), 1
    )
    own_copy.wait()
    row = jnp.sum(jnp.where(line == device - eight, group[...], 0), axis=0, keepdims=True)
    row = jnp.where(row < 0, jnp.int32(1 << 30), row)
    before = jnp.zeros((devices, 128), F32)
    for tile in range(total // 128):
        before = before + jnp.where(row[:, tile * 128:(tile + 1) * 128] < below, 1.0, 0.0)
    ones = jnp.ones((128, 128), BF16)
    before = jnp.dot(before.astype(BF16), ones, preferred_element_type=F32)
    first = jnp.sum(jnp.where(same, before, 0.0), axis=0, keepdims=True).astype(jnp.int32)
    firsts[...] = jnp.broadcast_to(first, firsts.shape)
    starts_copy = pltpu.make_async_copy(firsts, starts, sems.at[2])
    starts_copy.start()
    ints_copy.wait()
    for step in range(total // chunk):
        at = pl.ds(step * chunk, chunk)
        slots[at, :] = lax.dot_general(eye, staged[:, at], NT, preferred_element_type=F32)
    starts_copy.wait()
    pieces = sems.shape[0] - 3
    each = devices // pieces
    copies = []
    for piece in range(pieces):
        for dest in range(piece * each, (piece + 1) * each):
            start = starts[0, dest]
            aligned = pl.multiple_of((start >> 3) << 3, 8)
            window = slots[pl.ds(aligned, capacity + 8), :]
            window = pltpu.roll(window, capacity + 8 - (start & 7), 0)
            windows[dest] = window[:capacity].astype(BF16)
        at = pl.ds(piece * each, each)
        copies.append(pltpu.make_async_copy(windows.at[at], out.at[at], sems.at[3 + piece]))
        copies[-1].start()
    for copy in copies:
        copy.wait()


def order_kernel(capacity, width, base_ref, owned, out, held, sem):
    copy = pltpu.make_async_copy(owned, held, sem)
    copy.start()
    base = base_ref[0]
    holders, total = owned.shape
    beyond = jnp.int32(1 << 30)
    copy.wait()
    table = held[...]
    table = jnp.where(table < 0, beyond, table - base)
    below = jnp.zeros((holders, 128), F32)
    for tile in range(total // 128):
        below = below + jnp.where(table[:, tile * 128:(tile + 1) * 128] < 0, 1.0, 0.0)
    ones = jnp.ones((128, 128), BF16)
    start = jnp.dot(below.astype(BF16), ones, preferred_element_type=F32).astype(jnp.int32)
    window = jnp.concatenate([table, jnp.full((holders, 128), beyond, jnp.int32)], axis=1)
    shift = total // 2
    while shift >= 128:
        keep = shift + 128
        taken = (start & shift) != 0
        taken = jnp.concatenate([taken] * (keep // 128), axis=1)
        window = jnp.where(taken, window[:, shift:shift + keep], window[:, :keep])
        shift //= 2
    while shift >= 1:
        taken = (start & shift) != 0
        taken = jnp.concatenate([taken, taken], axis=1)
        window = jnp.where(taken, pltpu.roll(window, 256 - shift, 1), window)
        shift //= 2
    lane = lax.broadcasted_iota(jnp.int32, (holders, 128), 1)
    spread = jnp.where(lane < capacity, window[:, :128], 0)
    shift = capacity
    while shift < 128:
        spread = spread + pltpu.roll(spread, shift, 1)
        shift *= 2
    each = 128 // capacity
    mine = lax.broadcasted_iota(jnp.int32, (each, 128), 0)
    mine = mine == lax.broadcasted_iota(jnp.int32, (each, 128), 1) // capacity
    columns = jnp.concatenate(
        [
            jnp.sum(jnp.where(mine, spread[at:at + each], 0), axis=0, keepdims=True)
            for at in range(0, holders, each)
        ],
        axis=1,
    )
    out[...] = jnp.broadcast_to(columns, out.shape)


def multiply_kernel(
    where_ref, received, columns, amps0, amps1, amps2, amps3, kept, given, left, amps, sems
):
    group, core = where_ref[0], where_ref[1]
    holders, capacity, pairs = received.shape
    blocks, width, _ = amps.shape
    copies = []
    for step, part in enumerate((amps0, amps1, amps2, amps3)):
        target = amps.at[lax.rem(group + step, blocks)]
        copies.append(pltpu.make_async_copy(part, target, sems.at[step]))
        copies[-1].start()
    new = lax.broadcasted_iota(jnp.int32, (pairs, pairs), 0)
    old = lax.broadcasted_iota(jnp.int32, (pairs, pairs), 1)
    half = pairs // 2
    chips = half // 2
    side = jnp.where(new < half, core, 1 - core)
    in_half = jnp.where(new < half, new, new - half)
    row = jnp.where(in_half < chips, 0, 1)
    chip = jnp.where(in_half < chips, in_half, in_half - chips)
    pick = jnp.where(old == 4 * chip + 2 * side + row, 1.0, 0.0).astype(BF16)
    slot_count = holders * capacity
    slots = lax.dot_general(
        pick, received[...].reshape(slot_count, pairs), NT, preferred_element_type=F32
    ).astype(BF16)
    place = columns[0:1, :]
    chunk = 256
    for step in range(width // chunk):
        wanted = lax.broadcasted_iota(jnp.int32, (chunk, slot_count), 0) + step * chunk
        order = jnp.where(wanted == place, 1.0, 0.0).astype(BF16)
        left[:, step * chunk:(step + 1) * chunk] = lax.dot_general(
            slots, order, NT, preferred_element_type=F32
        ).astype(BF16)
    for copy in copies:
        copy.wait()
    for block in range(blocks):
        product = jnp.dot(left[...], amps[block], preferred_element_type=F32)
        for target, at in ((kept, 0), (given, half)):
            for r in range(2):
                for h in range(2):
                    target[pl.ds(r * 8 + 2 * block + h, chips, stride=16), :] = product[
                        at + r * chips:at + (r + 1) * chips, h * 128:(h + 1) * 128
                    ]


def pack(where, owned_columns, ladder_ints, devices, capacity):
    pairs, total = ladder_ints.shape
    return pl.pallas_call(
        pack_kernel,
        out_shape=jax.ShapeDtypeStruct((devices, capacity, pairs), BF16),
        in_specs=[SMEM, HBM, HBM],
        out_specs=HBM,
        scratch_shapes=[
            pltpu.VMEM((8, total), jnp.int32),
            pltpu.VMEM((pairs, total), BF16),
            pltpu.VMEM((total + capacity + 8, pairs), F32),
            pltpu.VMEM((8, 128), jnp.int32),
            pltpu.SMEM((8, 128), jnp.int32),
            pltpu.VMEM((devices, capacity, pairs), BF16),
            pltpu.SemaphoreType.DMA((11,)),
        ],
        compiler_params=pltpu.CompilerParams(vmem_limit_bytes=VMEM_LIMIT),
        name="pack",
    )(where, in_hbm(owned_columns), in_hbm(ladder_ints))


def order(base, owned_columns, capacity, width):
    holders, _ = owned_columns.shape
    return pl.pallas_call(
        lambda *refs: order_kernel(capacity, width, *refs),
        out_shape=jax.ShapeDtypeStruct((8, holders * capacity), jnp.int32),
        in_specs=[SMEM, HBM],
        out_specs=VMEM,
        scratch_shapes=[
            pltpu.VMEM(owned_columns.shape, jnp.int32),
            pltpu.SemaphoreType.DMA,
        ],
        compiler_params=pltpu.CompilerParams(vmem_limit_bytes=VMEM_LIMIT),
        name="order",
        cost_estimate=pl.CostEstimate(flops=15_000_000_000, bytes_accessed=1_000_000, transcendentals=0),
    )(base, in_hbm(owned_columns))


def multiply(where, received, columns, amps0, amps1, amps2, amps3):
    pairs = received.shape[2]
    width, pairs_ij = amps0.shape
    out = jax.ShapeDtypeStruct((pairs // 2 * 4 * pairs_ij // 128, 128), F32)
    return pl.pallas_call(
        multiply_kernel,
        out_shape=[out, out],
        in_specs=[SMEM, VMEM, VMEM] + [ANY] * 4,
        out_specs=[VMEM, VMEM],
        scratch_shapes=[
            pltpu.VMEM((pairs, width), BF16),
            pltpu.VMEM((4, width, pairs_ij), BF16),
            pltpu.SemaphoreType.DMA((4,)),
        ],
        compiler_params=pltpu.CompilerParams(vmem_limit_bytes=VMEM_LIMIT),
        name="multiply",
    )(where, received, columns, amps0, amps1, amps2, amps3)


SCALE = 2.0 ** 22


def squeeze(value):
    return (jnp.sign(value) * jnp.sqrt(jnp.abs(value) * SCALE)).astype(jnp.float16)


def unsqueeze(root):
    root = root.astype(F32)
    return root * jnp.abs(root) * (1.0 / SCALE)


def body(amplitudes, owned_columns, ladder_ints):
    device = lax.axis_index("cd")
    group = lax.axis_index("ij")
    devices_cd = lax.axis_size("cd")
    groups = lax.axis_size("ij")
    width = amplitudes.shape[0]
    capacity = 2 * width // devices_cd

    own = jnp.stack([device, jnp.int32(width)]).astype(jnp.int32)
    outgoing = pack(own, owned_columns, ladder_ints, devices_cd, capacity)
    incoming = lax.all_to_all(outgoing, "cd", split_axis=0, concat_axis=0, tiled=True)
    def from_group(value, step):
        return lax.ppermute(value, "ij", [((i + step) % groups, i) for i in range(groups)])

    amps2 = from_group(amplitudes, 2)
    base, amps2 = lax.optimization_barrier(((device * width)[None].astype(jnp.int32), amps2))
    columns = order(base, owned_columns, capacity, width)
    later, columns = lax.optimization_barrier((amplitudes, columns))
    others = [from_group(later, 1), amps2, from_group(later, 3)]
    where = jnp.stack([group, lax.rem(device, 2)]).astype(jnp.int32)
    kept, given = multiply(where, incoming, columns, amplitudes, *others)
    taken = lax.ppermute(given, "cd", [(i, i ^ 1) for i in range(devices_cd)])
    both = squeeze(kept + taken).reshape(devices_cd // 2, 16, 128)
    same_core = [[2 * k + c for k in range(devices_cd // 2)] for c in range(2)]
    shares = lax.all_to_all(both, "cd", 0, 0, tiled=True, axis_index_groups=same_core)
    summed = jnp.sum(unsqueeze(shares), axis=0)
    return summed.astype(BF16).reshape(2, 1024)


def solution(mesh):
    return jax.shard_map(
        body,
        mesh=mesh,
        in_specs=(P("cd", "ij"), P(), P("ij", "cd")),
        out_specs=P(("ij", "cd"), None),
        check_vma=False,
    )
```

```python
import jax
import jax.numpy as jnp
from jax import lax
from jax.experimental import pallas as pl
from jax.experimental.pallas import tpu as pltpu
from jax.sharding import PartitionSpec as P

F32 = jnp.float32
BF16 = jnp.bfloat16
NT = (((1,), (1,)), ((), ()))
VMEM_LIMIT = 24 * 1024 * 1024
VMEM = pl.BlockSpec(memory_space=pltpu.VMEM)
SMEM = pl.BlockSpec(memory_space=pltpu.SMEM)
ANY = pl.BlockSpec(memory_space=pl.ANY)
HBM = pl.BlockSpec(memory_space=pltpu.HBM)


def in_hbm(value):
    return pltpu.with_memory_space_constraint(value, pltpu.HBM)


def pack_kernel(where_ref, owned, ints, out, group, staged, slots, firsts, starts, windows, sems):
    device, width = where_ref[0], where_ref[1]
    devices, capacity, _ = out.shape
    total, chunk = ints.shape[1], 256
    eight = pl.multiple_of((device >> 3) << 3, 8)
    own_copy = pltpu.make_async_copy(owned.at[pl.ds(eight, 8)], group, sems.at[0])
    own_copy.start()
    ints_copy = pltpu.make_async_copy(ints, staged, sems.at[1])
    ints_copy.start()
    slots[pl.ds(total, capacity + 8), :] = jnp.zeros((capacity + 8, slots.shape[1]), F32)
    rows = lax.broadcasted_iota(jnp.int32, (chunk, chunk), 0)
    cols = lax.broadcasted_iota(jnp.int32, (chunk, chunk), 1)
    eye = jnp.where(rows == cols, 1.0, 0.0).astype(BF16)
    line = lax.broadcasted_iota(jnp.int32, group.shape, 0)
    below = lax.broadcasted_iota(jnp.int32, (devices, 128), 0) * width
    same = lax.broadcasted_iota(jnp.int32, (devices, 128), 0) == lax.broadcasted_iota(
        jnp.int32, (devices, 128), 1
    )
    own_copy.wait()
    row = jnp.sum(jnp.where(line == device - eight, group[...], 0), axis=0, keepdims=True)
    row = jnp.where(row < 0, jnp.int32(1 << 30), row)
    before = jnp.zeros((devices, 128), F32)
    for tile in range(total // 128):
        before = before + jnp.where(row[:, tile * 128:(tile + 1) * 128] < below, 1.0, 0.0)
    ones = jnp.ones((128, 128), BF16)
    before = jnp.dot(before.astype(BF16), ones, preferred_element_type=F32)
    first = jnp.sum(jnp.where(same, before, 0.0), axis=0, keepdims=True).astype(jnp.int32)
    firsts[...] = jnp.broadcast_to(first, firsts.shape)
    starts_copy = pltpu.make_async_copy(firsts, starts, sems.at[2])
    starts_copy.start()
    ints_copy.wait()
    for step in range(total // chunk):
        at = pl.ds(step * chunk, chunk)
        slots[at, :] = lax.dot_general(eye, staged[:, at], NT, preferred_element_type=F32)
    starts_copy.wait()
    pieces = sems.shape[0] - 3
    each = devices // pieces
    copies = []
    for piece in range(pieces):
        for dest in range(piece * each, (piece + 1) * each):
            start = starts[0, dest]
            aligned = pl.multiple_of((start >> 3) << 3, 8)
            window = slots[pl.ds(aligned, capacity + 8), :]
            window = pltpu.roll(window, capacity + 8 - (start & 7), 0)
            windows[dest] = window[:capacity].astype(BF16)
        at = pl.ds(piece * each, each)
        copies.append(pltpu.make_async_copy(windows.at[at], out.at[at], sems.at[3 + piece]))
        copies[-1].start()
    for copy in copies:
        copy.wait()


def order_kernel(capacity, width, base_ref, owned, place_out, offsets_out, held, sem):
    copy = pltpu.make_async_copy(owned, held, sem)
    copy.start()
    base = base_ref[0]
    holders, total = owned.shape
    beyond = jnp.int32(1 << 30)
    copy.wait()
    table = held[...]
    table = jnp.where(table < 0, beyond, table - base)
    below = jnp.zeros((holders, 128), F32)
    ended = jnp.zeros((holders, 128), F32)
    for tile in range(total // 128):
        part = table[:, tile * 128:(tile + 1) * 128]
        below = below + jnp.where(part < 0, 1.0, 0.0)
        ended = ended + jnp.where(part < width, 1.0, 0.0)
    ones = jnp.ones((128, 128), BF16)
    below = jnp.dot(below.astype(BF16), ones, preferred_element_type=F32)
    ended = jnp.dot(ended.astype(BF16), ones, preferred_element_type=F32)
    counts = (ended - below).astype(BF16)
    rows = lax.broadcasted_iota(jnp.int32, (holders, holders), 0)
    cols = lax.broadcasted_iota(jnp.int32, (holders, holders), 1)
    earlier = jnp.where(cols < rows, 1.0, 0.0).astype(BF16)
    first = jnp.dot(earlier, counts, preferred_element_type=F32).astype(jnp.int32)
    offsets = jnp.sum(jnp.where(rows == cols, first, 0), axis=0, keepdims=True)
    offsets_out[...] = jnp.broadcast_to(offsets, offsets_out.shape)
    start = below.astype(jnp.int32)
    window = jnp.concatenate([table, jnp.full((holders, 128), beyond, jnp.int32)], axis=1)
    shift = total // 2
    while shift >= 128:
        keep = shift + 128
        taken = (start & shift) != 0
        taken = jnp.concatenate([taken] * (keep // 128), axis=1)
        window = jnp.where(taken, window[:, shift:shift + keep], window[:, :keep])
        shift //= 2
    while shift >= 1:
        taken = (start & shift) != 0
        taken = jnp.concatenate([taken, taken], axis=1)
        window = jnp.where(taken, pltpu.roll(window, 256 - shift, 1), window)
        shift //= 2
    column = lax.broadcasted_iota(jnp.int32, (holders, width), 1)
    place = jnp.zeros((holders, width), jnp.int32)
    for slot in range(capacity):
        here = window[:, slot:slot + 1] == column
        place = place + jnp.where(here, first[:, :1] + slot, 0)
    place = jnp.sum(place, axis=0, keepdims=True)
    place_out[...] = jnp.broadcast_to(place, place_out.shape)


def arrange_kernel(place, *refs):
    blocks, outs = refs[:len(refs) // 2], refs[len(refs) // 2:]
    width = place.shape[1]
    chunk = 256
    where_to = place[0:1, :]
    for step in range(width // chunk):
        wanted = lax.broadcasted_iota(jnp.int32, (chunk, width), 0) + step * chunk
        pick = jnp.where(wanted == where_to, 1.0, 0.0).astype(BF16)
        for block, out in zip(blocks, outs):
            out[pl.ds(step * chunk, chunk), :] = jnp.dot(
                pick, block[...], preferred_element_type=F32
            ).astype(BF16)


def multiply_kernel(
    where_ref, offsets, received, amps0, amps1, amps2, amps3, given, left_kept, rows_ref, left
):
    group, core = where_ref[0], where_ref[1]
    holders, capacity, pairs = received.shape
    width = amps0.shape[0]
    line = lax.broadcasted_iota(jnp.int32, (8, pairs), 0)
    blank = jnp.zeros((8, pairs), F32)
    for holder in range(holders):
        start = offsets[0, holder]
        aligned = pl.multiple_of((start >> 3) << 3, 8)
        window = jnp.concatenate([received[holder].astype(F32), blank], axis=0)
        window = pltpu.roll(window, start & 7, 0)
        pltpu.store(rows_ref.at[pl.ds(aligned, 8)], window[:8], mask=line >= (start & 7))
        rows_ref[pl.ds(aligned + 8, capacity), :] = window[8:]
    new = lax.broadcasted_iota(jnp.int32, (pairs, pairs), 0)
    old = lax.broadcasted_iota(jnp.int32, (pairs, pairs), 1)
    half = pairs // 2
    chips = half // 2
    side = jnp.where(new < half, core, 1 - core)
    in_half = jnp.where(new < half, new, new - half)
    row = jnp.where(in_half < chips, 0, 1)
    chip = jnp.where(in_half < chips, in_half, in_half - chips)
    pick = jnp.where(old == 4 * chip + 2 * side + row, 1.0, 0.0).astype(BF16)
    chunk = 256
    for step in range(width // chunk):
        left[:, step * chunk:(step + 1) * chunk] = lax.dot_general(
            pick,
            rows_ref[pl.ds(step * chunk, chunk), :].astype(BF16),
            NT,
            preferred_element_type=F32,
        ).astype(BF16)
    left_kept[...] = left[:half, :]
    cut_product(group, left[half:, :], (amps0, amps1, amps2, amps3), given)


def cut_product(group, left, blocks, target):
    chips = left.shape[0] // 2
    for step, amps in enumerate(blocks):
        block = lax.rem(group + step, 4)
        product = jnp.dot(left, amps[...], preferred_element_type=F32)
        for r in range(2):
            for h in range(2):
                target[pl.ds(r * 8 + 2 * block + h, chips, stride=16), :] = product[
                    r * chips:(r + 1) * chips, h * 128:(h + 1) * 128
                ]


def keep_kernel(where_ref, left, amps0, amps1, amps2, amps3, kept):
    cut_product(where_ref[0], left[...], (amps0, amps1, amps2, amps3), kept)


def pack(where, owned_columns, ladder_ints, devices, capacity):
    pairs, total = ladder_ints.shape
    return pl.pallas_call(
        pack_kernel,
        out_shape=jax.ShapeDtypeStruct((devices, capacity, pairs), BF16),
        in_specs=[SMEM, HBM, HBM],
        out_specs=HBM,
        scratch_shapes=[
            pltpu.VMEM((8, total), jnp.int32),
            pltpu.VMEM((pairs, total), BF16),
            pltpu.VMEM((total + capacity + 8, pairs), F32),
            pltpu.VMEM((8, 128), jnp.int32),
            pltpu.SMEM((8, 128), jnp.int32),
            pltpu.VMEM((devices, capacity, pairs), BF16),
            pltpu.SemaphoreType.DMA((11,)),
        ],
        compiler_params=pltpu.CompilerParams(vmem_limit_bytes=VMEM_LIMIT),
        name="pack",
    )(where, in_hbm(owned_columns), in_hbm(ladder_ints))


def order(base, owned_columns, capacity, width):
    holders, _ = owned_columns.shape
    return pl.pallas_call(
        lambda *refs: order_kernel(capacity, width, *refs),
        out_shape=[
            jax.ShapeDtypeStruct((8, width), jnp.int32),
            jax.ShapeDtypeStruct((8, holders), jnp.int32),
        ],
        in_specs=[SMEM, HBM],
        out_specs=[VMEM, VMEM],
        scratch_shapes=[
            pltpu.VMEM(owned_columns.shape, jnp.int32),
            pltpu.SemaphoreType.DMA,
        ],
        compiler_params=pltpu.CompilerParams(vmem_limit_bytes=VMEM_LIMIT),
        name="order",
        cost_estimate=pl.CostEstimate(
            flops=15_000_000_000, bytes_accessed=1_000_000, transcendentals=0
        ),
    )(base, in_hbm(owned_columns))


def arrange(place, *blocks):
    return pl.pallas_call(
        arrange_kernel,
        out_shape=[jax.ShapeDtypeStruct(block.shape, block.dtype) for block in blocks],
        in_specs=[VMEM] * (1 + len(blocks)),
        out_specs=[VMEM] * len(blocks),
        compiler_params=pltpu.CompilerParams(vmem_limit_bytes=VMEM_LIMIT),
        name="arrange",
        cost_estimate=pl.CostEstimate(
            flops=2_000_000_000, bytes_accessed=2_000_000, transcendentals=0
        ),
    )(place, *blocks)


def multiply(where, offsets, received, *amps):
    _, capacity, pairs = received.shape
    width, pairs_ij = amps[0].shape
    return pl.pallas_call(
        multiply_kernel,
        out_shape=[
            jax.ShapeDtypeStruct((pairs // 2 * 4 * pairs_ij // 128, 128), F32),
            jax.ShapeDtypeStruct((pairs // 2, width), BF16),
        ],
        in_specs=[SMEM, SMEM] + [VMEM] * 5,
        out_specs=[VMEM, VMEM],
        scratch_shapes=[
            pltpu.VMEM((width + capacity + 8, pairs), F32),
            pltpu.VMEM((pairs, width), BF16),
        ],
        compiler_params=pltpu.CompilerParams(vmem_limit_bytes=VMEM_LIMIT),
        name="multiply",
    )(where, offsets, received, *amps)


def keep(where, left, *amps):
    half, _ = left.shape
    _, pairs_ij = amps[0].shape
    return pl.pallas_call(
        keep_kernel,
        out_shape=jax.ShapeDtypeStruct((half * 4 * pairs_ij // 128, 128), F32),
        in_specs=[SMEM] + [VMEM] * 5,
        out_specs=VMEM,
        compiler_params=pltpu.CompilerParams(vmem_limit_bytes=VMEM_LIMIT),
        name="keep",
        cost_estimate=pl.CostEstimate(
            flops=1_000_000_000, bytes_accessed=3_000_000, transcendentals=0
        ),
    )(where, left, *amps)


SCALE = 2.0 ** 22


def squeeze(value):
    return (jnp.sign(value) * jnp.sqrt(jnp.abs(value) * SCALE)).astype(jnp.float16)


def unsqueeze(root):
    root = root.astype(F32)
    return root * jnp.abs(root) * (1.0 / SCALE)


def body(amplitudes, owned_columns, ladder_ints):
    device = lax.axis_index("cd")
    group = lax.axis_index("ij")
    devices_cd = lax.axis_size("cd")
    groups = lax.axis_size("ij")
    width = amplitudes.shape[0]
    capacity = 2 * width // devices_cd

    own = jnp.stack([device, jnp.int32(width)]).astype(jnp.int32)
    outgoing = pack(own, owned_columns, ladder_ints, devices_cd, capacity)
    incoming = lax.all_to_all(outgoing, "cd", split_axis=0, concat_axis=0, tiled=True)
    def from_group(value, step):
        return lax.ppermute(value, "ij", [((i + step) % groups, i) for i in range(groups)])

    amps2 = from_group(amplitudes, 2)
    place, offsets = order((device * width)[None].astype(jnp.int32), owned_columns, capacity, width)
    later, amps2 = lax.optimization_barrier((amplitudes, amps2))
    amps1, amps3 = from_group(later, 1), from_group(later, 3)
    amps0, amps2 = arrange(place, amplitudes, amps2)
    amps1, amps3 = arrange(place, amps1, amps3)
    where = jnp.stack([group, lax.rem(device, 2)]).astype(jnp.int32)
    given, left = multiply(where, offsets, incoming, amps0, amps1, amps2, amps3)
    kept = keep(where, left, amps0, amps1, amps2, amps3)
    taken = lax.ppermute(given, "cd", [(i, i ^ 1) for i in range(devices_cd)])
    both = squeeze(kept + taken).reshape(devices_cd // 2, 16, 128)
    same_core = [[2 * k + c for k in range(devices_cd // 2)] for c in range(2)]
    shares = lax.all_to_all(both, "cd", 0, 0, tiled=True, axis_index_groups=same_core)
    summed = jnp.sum(unsqueeze(shares), axis=0)
    return summed.astype(BF16).reshape(2, 1024)


def solution(mesh):
    return jax.shard_map(
        body,
        mesh=mesh,
        in_specs=(P("cd", "ij"), P(), P("ij", "cd")),
        out_specs=P(("ij", "cd"), None),
        check_vma=False,
    )
```

```python
import jax
import jax.numpy as jnp
from jax import lax
from jax.experimental import pallas as pl
from jax.experimental.pallas import tpu as pltpu
from jax.sharding import PartitionSpec as P

F32 = jnp.float32
BF16 = jnp.bfloat16
NT = (((1,), (1,)), ((), ()))
VMEM_LIMIT = 24 * 1024 * 1024
VMEM = pl.BlockSpec(memory_space=pltpu.VMEM)
SMEM = pl.BlockSpec(memory_space=pltpu.SMEM)
ANY = pl.BlockSpec(memory_space=pl.ANY)
HBM = pl.BlockSpec(memory_space=pltpu.HBM)


def in_hbm(value):
    return pltpu.with_memory_space_constraint(value, pltpu.HBM)


def pack_kernel(width, owned, ints, out, group, staged, slots, firsts, starts, windows, sems):
    device = lax.axis_index("cd")
    devices, capacity, _ = out.shape
    total, chunk = ints.shape[1], 256
    eight = pl.multiple_of((device >> 3) << 3, 8)
    own_copy = pltpu.make_async_copy(owned.at[pl.ds(eight, 8)], group, sems.at[0])
    own_copy.start()
    ints_copy = pltpu.make_async_copy(ints, staged, sems.at[1])
    ints_copy.start()
    slots[pl.ds(total, capacity + 8), :] = jnp.zeros((capacity + 8, slots.shape[1]), F32)
    rows = lax.broadcasted_iota(jnp.int32, (chunk, chunk), 0)
    cols = lax.broadcasted_iota(jnp.int32, (chunk, chunk), 1)
    eye = jnp.where(rows == cols, 1.0, 0.0).astype(BF16)
    line = lax.broadcasted_iota(jnp.int32, group.shape, 0)
    below = lax.broadcasted_iota(jnp.int32, (devices, 128), 0) * width
    same = lax.broadcasted_iota(jnp.int32, (devices, 128), 0) == lax.broadcasted_iota(
        jnp.int32, (devices, 128), 1
    )
    own_copy.wait()
    row = jnp.sum(jnp.where(line == device - eight, group[...], 0), axis=0, keepdims=True)
    row = jnp.where(row < 0, jnp.int32(1 << 30), row)
    before = jnp.zeros((devices, 128), F32)
    for tile in range(total // 128):
        before = before + jnp.where(row[:, tile * 128:(tile + 1) * 128] < below, 1.0, 0.0)
    ones = jnp.ones((128, 128), BF16)
    before = jnp.dot(before.astype(BF16), ones, preferred_element_type=F32)
    first = jnp.sum(jnp.where(same, before, 0.0), axis=0, keepdims=True).astype(jnp.int32)
    firsts[...] = jnp.broadcast_to(first, firsts.shape)
    starts_copy = pltpu.make_async_copy(firsts, starts, sems.at[2])
    starts_copy.start()
    ints_copy.wait()
    for step in range(total // chunk):
        at = pl.ds(step * chunk, chunk)
        slots[at, :] = lax.dot_general(eye, staged[:, at], NT, preferred_element_type=F32)
    starts_copy.wait()
    pieces = sems.shape[0] - 3
    each = devices // pieces
    copies = []
    for piece in range(pieces):
        for dest in range(piece * each, (piece + 1) * each):
            start = starts[0, dest]
            aligned = pl.multiple_of((start >> 3) << 3, 8)
            window = slots[pl.ds(aligned, capacity + 8), :]
            window = pltpu.roll(window, capacity + 8 - (start & 7), 0)
            windows[dest] = window[:capacity].astype(BF16)
        at = pl.ds(piece * each, each)
        copies.append(pltpu.make_async_copy(windows.at[at], out.at[at], sems.at[3 + piece]))
        copies[-1].start()
    for copy in copies:
        copy.wait()


def order_kernel(capacity, width, owned, place_out, offsets_out, held, sem):
    copy = pltpu.make_async_copy(owned, held, sem)
    copy.start()
    base = lax.axis_index("cd") * width
    holders, total = owned.shape
    beyond = jnp.int32(1 << 30)
    copy.wait()
    table = held[...]
    table = jnp.where(table < 0, beyond, table - base)
    below = jnp.zeros((holders, 128), F32)
    ended = jnp.zeros((holders, 128), F32)
    for tile in range(total // 128):
        part = table[:, tile * 128:(tile + 1) * 128]
        below = below + jnp.where(part < 0, 1.0, 0.0)
        ended = ended + jnp.where(part < width, 1.0, 0.0)
    ones = jnp.ones((128, 128), BF16)
    below = jnp.dot(below.astype(BF16), ones, preferred_element_type=F32)
    ended = jnp.dot(ended.astype(BF16), ones, preferred_element_type=F32)
    counts = (ended - below).astype(BF16)
    rows = lax.broadcasted_iota(jnp.int32, (holders, holders), 0)
    cols = lax.broadcasted_iota(jnp.int32, (holders, holders), 1)
    earlier = jnp.where(cols < rows, 1.0, 0.0).astype(BF16)
    first = jnp.dot(earlier, counts, preferred_element_type=F32).astype(jnp.int32)
    offsets = jnp.sum(jnp.where(rows == cols, first, 0), axis=0, keepdims=True)
    offsets_out[...] = jnp.broadcast_to(offsets, offsets_out.shape)
    start = below.astype(jnp.int32)
    window = jnp.concatenate([table, jnp.full((holders, 128), beyond, jnp.int32)], axis=1)
    shift = total // 2
    while shift >= 128:
        keep = shift + 128
        taken = (start & shift) != 0
        taken = jnp.concatenate([taken] * (keep // 128), axis=1)
        window = jnp.where(taken, window[:, shift:shift + keep], window[:, :keep])
        shift //= 2
    while shift >= 1:
        taken = (start & shift) != 0
        taken = jnp.concatenate([taken, taken], axis=1)
        window = jnp.where(taken, pltpu.roll(window, 256 - shift, 1), window)
        shift //= 2
    column = lax.broadcasted_iota(jnp.int32, (holders, width), 1)
    place = jnp.zeros((holders, width), jnp.int32)
    for slot in range(capacity):
        here = window[:, slot:slot + 1] == column
        place = place + jnp.where(here, first[:, :1] + slot, 0)
    place = jnp.sum(place, axis=0, keepdims=True)
    place_out[...] = jnp.broadcast_to(place, place_out.shape)


def arrange_kernel(place, *refs):
    blocks, outs = refs[:len(refs) // 2], refs[len(refs) // 2:]
    width = place.shape[1]
    chunk = 256
    where_to = place[0:1, :]
    for step in range(width // chunk):
        wanted = lax.broadcasted_iota(jnp.int32, (chunk, width), 0) + step * chunk
        pick = jnp.where(wanted == where_to, 1.0, 0.0).astype(BF16)
        for block, out in zip(blocks, outs):
            out[pl.ds(step * chunk, chunk), :] = jnp.dot(
                pick, block[...], preferred_element_type=F32
            ).astype(BF16)


def multiply_kernel(
    offsets, received, amps0, amps1, amps2, amps3, given, left_kept, rows_ref, left
):
    group, core = lax.axis_index("ij"), lax.rem(lax.axis_index("cd"), 2)
    holders, capacity, pairs = received.shape
    width = amps0.shape[0]
    line = lax.broadcasted_iota(jnp.int32, (8, pairs), 0)
    blank = jnp.zeros((8, pairs), F32)
    for holder in range(holders):
        start = offsets[0, holder]
        aligned = pl.multiple_of((start >> 3) << 3, 8)
        window = jnp.concatenate([received[holder].astype(F32), blank], axis=0)
        window = pltpu.roll(window, start & 7, 0)
        pltpu.store(rows_ref.at[pl.ds(aligned, 8)], window[:8], mask=line >= (start & 7))
        rows_ref[pl.ds(aligned + 8, capacity), :] = window[8:]
    new = lax.broadcasted_iota(jnp.int32, (pairs, pairs), 0)
    old = lax.broadcasted_iota(jnp.int32, (pairs, pairs), 1)
    half = pairs // 2
    chips = half // 2
    side = jnp.where(new < half, core, 1 - core)
    in_half = jnp.where(new < half, new, new - half)
    row = jnp.where(in_half < chips, 0, 1)
    chip = jnp.where(in_half < chips, in_half, in_half - chips)
    pick = jnp.where(old == 4 * chip + 2 * side + row, 1.0, 0.0).astype(BF16)
    chunk = 256
    for step in range(width // chunk):
        left[:, step * chunk:(step + 1) * chunk] = lax.dot_general(
            pick,
            rows_ref[pl.ds(step * chunk, chunk), :].astype(BF16),
            NT,
            preferred_element_type=F32,
        ).astype(BF16)
    left_kept[...] = left[:half, :]
    cut_product(group, left[half:, :], (amps0, amps1, amps2, amps3), given)


def cut_product(group, left, blocks, target):
    chips = left.shape[0] // 2
    for step, amps in enumerate(blocks):
        block = lax.rem(group + step, 4)
        product = jnp.dot(left, amps[...], preferred_element_type=F32)
        for r in range(2):
            for h in range(2):
                target[pl.ds(r * 8 + 2 * block + h, chips, stride=16), :] = product[
                    r * chips:(r + 1) * chips, h * 128:(h + 1) * 128
                ]


def keep_kernel(left, amps0, amps1, amps2, amps3, kept):
    cut_product(lax.axis_index("ij"), left[...], (amps0, amps1, amps2, amps3), kept)


def pack(owned_columns, ladder_ints, devices, capacity, width):
    pairs, total = ladder_ints.shape
    return pl.pallas_call(
        lambda *refs: pack_kernel(width, *refs),
        out_shape=jax.ShapeDtypeStruct((devices, capacity, pairs), BF16),
        in_specs=[HBM, HBM],
        out_specs=HBM,
        scratch_shapes=[
            pltpu.VMEM((8, total), jnp.int32),
            pltpu.VMEM((pairs, total), BF16),
            pltpu.VMEM((total + capacity + 8, pairs), F32),
            pltpu.VMEM((8, 128), jnp.int32),
            pltpu.SMEM((8, 128), jnp.int32),
            pltpu.VMEM((devices, capacity, pairs), BF16),
            pltpu.SemaphoreType.DMA((11,)),
        ],
        compiler_params=pltpu.CompilerParams(vmem_limit_bytes=VMEM_LIMIT),
        name="pack",
    )(in_hbm(owned_columns), in_hbm(ladder_ints))


def order(owned_columns, capacity, width):
    holders, _ = owned_columns.shape
    return pl.pallas_call(
        lambda *refs: order_kernel(capacity, width, *refs),
        out_shape=[
            jax.ShapeDtypeStruct((8, width), jnp.int32),
            jax.ShapeDtypeStruct((8, holders), jnp.int32),
        ],
        in_specs=[HBM],
        out_specs=[VMEM, VMEM],
        scratch_shapes=[
            pltpu.VMEM(owned_columns.shape, jnp.int32),
            pltpu.SemaphoreType.DMA,
        ],
        compiler_params=pltpu.CompilerParams(vmem_limit_bytes=VMEM_LIMIT),
        name="order",
        cost_estimate=pl.CostEstimate(
            flops=15_000_000_000, bytes_accessed=1_000_000, transcendentals=0
        ),
    )(in_hbm(owned_columns))


def arrange(place, *blocks):
    return pl.pallas_call(
        arrange_kernel,
        out_shape=[jax.ShapeDtypeStruct(block.shape, block.dtype) for block in blocks],
        in_specs=[VMEM] * (1 + len(blocks)),
        out_specs=[VMEM] * len(blocks),
        compiler_params=pltpu.CompilerParams(vmem_limit_bytes=VMEM_LIMIT),
        name="arrange",
        cost_estimate=pl.CostEstimate(
            flops=2_000_000_000, bytes_accessed=2_000_000, transcendentals=0
        ),
    )(place, *blocks)


def multiply(offsets, received, *amps):
    _, capacity, pairs = received.shape
    width, pairs_ij = amps[0].shape
    return pl.pallas_call(
        multiply_kernel,
        out_shape=[
            jax.ShapeDtypeStruct((pairs // 2 * 4 * pairs_ij // 128, 128), F32),
            jax.ShapeDtypeStruct((pairs // 2, width), BF16),
        ],
        in_specs=[SMEM] + [VMEM] * 5,
        out_specs=[VMEM, VMEM],
        scratch_shapes=[
            pltpu.VMEM((width + capacity + 8, pairs), F32),
            pltpu.VMEM((pairs, width), BF16),
        ],
        compiler_params=pltpu.CompilerParams(vmem_limit_bytes=VMEM_LIMIT),
        name="multiply",
    )(offsets, received, *amps)


def keep(left, *amps):
    half, _ = left.shape
    _, pairs_ij = amps[0].shape
    return pl.pallas_call(
        keep_kernel,
        out_shape=jax.ShapeDtypeStruct((half * 4 * pairs_ij // 128, 128), F32),
        in_specs=[VMEM] * 5,
        out_specs=VMEM,
        compiler_params=pltpu.CompilerParams(vmem_limit_bytes=VMEM_LIMIT),
        name="keep",
        cost_estimate=pl.CostEstimate(
            flops=1_000_000_000, bytes_accessed=3_000_000, transcendentals=0
        ),
    )(left, *amps)


SCALE = 2.0 ** 22


def squeeze(value):
    return (jnp.sign(value) * jnp.sqrt(jnp.abs(value) * SCALE)).astype(jnp.float16)


def unsqueeze(root):
    root = root.astype(F32)
    return root * jnp.abs(root) * (1.0 / SCALE)


def body(amplitudes, owned_columns, ladder_ints):
    devices_cd = lax.axis_size("cd")
    groups = lax.axis_size("ij")
    width = amplitudes.shape[0]
    capacity = 2 * width // devices_cd

    outgoing = pack(owned_columns, ladder_ints, devices_cd, capacity, width)
    incoming = lax.all_to_all(outgoing, "cd", split_axis=0, concat_axis=0, tiled=True)
    def from_group(value, step):
        return lax.ppermute(value, "ij", [((i + step) % groups, i) for i in range(groups)])

    amps2 = from_group(amplitudes, 2)
    place, offsets = order(owned_columns, capacity, width)
    later, amps2 = lax.optimization_barrier((amplitudes, amps2))
    amps1, amps3 = from_group(later, 1), from_group(later, 3)
    amps0, amps2 = arrange(place, amplitudes, amps2)
    amps1, amps3 = arrange(place, amps1, amps3)
    given, left = multiply(offsets, incoming, amps0, amps1, amps2, amps3)
    kept = keep(left, amps0, amps1, amps2, amps3)
    taken = lax.ppermute(given, "cd", [(i, i ^ 1) for i in range(devices_cd)])
    both = squeeze(kept + taken).reshape(devices_cd // 2, 16, 128)
    same_core = [[2 * k + c for k in range(devices_cd // 2)] for c in range(2)]
    shares = lax.all_to_all(both, "cd", 0, 0, tiled=True, axis_index_groups=same_core)
    summed = jnp.sum(unsqueeze(shares), axis=0)
    return summed.astype(BF16).reshape(2, 1024)


def solution(mesh):
    return jax.shard_map(
        body,
        mesh=mesh,
        in_specs=(P("cd", "ij"), P(), P("ij", "cd")),
        out_specs=P(("ij", "cd"), None),
        check_vma=False,
    )
```

```python
import jax
import jax.numpy as jnp
from jax import lax
from jax.experimental import pallas as pl
from jax.experimental.pallas import tpu as pltpu
from jax.sharding import PartitionSpec as P

F32 = jnp.float32
BF16 = jnp.bfloat16
NT = (((1,), (1,)), ((), ()))
VMEM_LIMIT = 24 * 1024 * 1024
VMEM = pl.BlockSpec(memory_space=pltpu.VMEM)
SMEM = pl.BlockSpec(memory_space=pltpu.SMEM)
ANY = pl.BlockSpec(memory_space=pl.ANY)
HBM = pl.BlockSpec(memory_space=pltpu.HBM)


def in_hbm(value):
    return pltpu.with_memory_space_constraint(value, pltpu.HBM)


def pack_kernel(width, owned, ints, out, group, staged, slots, firsts, starts, windows, sems):
    device = lax.axis_index("cd")
    devices, capacity, _ = out.shape
    total, chunk = ints.shape[1], 256
    eight = pl.multiple_of((device >> 3) << 3, 8)
    own_copy = pltpu.make_async_copy(owned.at[pl.ds(eight, 8)], group, sems.at[0])
    own_copy.start()
    ints_copy = pltpu.make_async_copy(ints, staged, sems.at[1])
    ints_copy.start()
    slots[pl.ds(total, capacity + 8), :] = jnp.zeros((capacity + 8, slots.shape[1]), F32)
    rows = lax.broadcasted_iota(jnp.int32, (chunk, chunk), 0)
    cols = lax.broadcasted_iota(jnp.int32, (chunk, chunk), 1)
    eye = jnp.where(rows == cols, 1.0, 0.0).astype(BF16)
    line = lax.broadcasted_iota(jnp.int32, group.shape, 0)
    below = lax.broadcasted_iota(jnp.int32, (devices, 128), 0) * width
    same = lax.broadcasted_iota(jnp.int32, (devices, 128), 0) == lax.broadcasted_iota(
        jnp.int32, (devices, 128), 1
    )
    own_copy.wait()
    row = jnp.sum(jnp.where(line == device - eight, group[...], 0), axis=0, keepdims=True)
    row = jnp.where(row < 0, jnp.int32(1 << 30), row)
    before = jnp.zeros((devices, 128), F32)
    for tile in range(total // 128):
        before = before + jnp.where(row[:, tile * 128:(tile + 1) * 128] < below, 1.0, 0.0)
    ones = jnp.ones((128, 128), BF16)
    before = jnp.dot(before.astype(BF16), ones, preferred_element_type=F32)
    first = jnp.sum(jnp.where(same, before, 0.0), axis=0, keepdims=True).astype(jnp.int32)
    firsts[...] = jnp.broadcast_to(first, firsts.shape)
    starts_copy = pltpu.make_async_copy(firsts, starts, sems.at[2])
    starts_copy.start()
    ints_copy.wait()
    for step in range(total // chunk):
        at = pl.ds(step * chunk, chunk)
        slots[at, :] = lax.dot_general(eye, staged[:, at], NT, preferred_element_type=F32)
    starts_copy.wait()
    pieces = sems.shape[0] - 3
    each = devices // pieces
    copies = []
    for piece in range(pieces):
        for dest in range(piece * each, (piece + 1) * each):
            start = starts[0, dest]
            aligned = pl.multiple_of((start >> 3) << 3, 8)
            window = slots[pl.ds(aligned, capacity + 8), :]
            window = pltpu.roll(window, capacity + 8 - (start & 7), 0)
            windows[dest] = window[:capacity].astype(BF16)
        at = pl.ds(piece * each, each)
        copies.append(pltpu.make_async_copy(windows.at[at], out.at[at], sems.at[3 + piece]))
        copies[-1].start()
    for copy in copies:
        copy.wait()


def order_kernel(capacity, width, owned, place_out, offsets_out, held, sem):
    copy = pltpu.make_async_copy(owned, held, sem)
    copy.start()
    base = lax.axis_index("cd") * width
    holders, total = owned.shape
    beyond = jnp.int32(1 << 30)
    copy.wait()
    table = held[...]
    table = jnp.where(table < 0, beyond, table - base)
    below = jnp.zeros((holders, 128), F32)
    ended = jnp.zeros((holders, 128), F32)
    for tile in range(total // 128):
        part = table[:, tile * 128:(tile + 1) * 128]
        below = below + jnp.where(part < 0, 1.0, 0.0)
        ended = ended + jnp.where(part < width, 1.0, 0.0)
    ones = jnp.ones((128, 128), BF16)
    below = jnp.dot(below.astype(BF16), ones, preferred_element_type=F32)
    ended = jnp.dot(ended.astype(BF16), ones, preferred_element_type=F32)
    counts = (ended - below).astype(BF16)
    rows = lax.broadcasted_iota(jnp.int32, (holders, holders), 0)
    cols = lax.broadcasted_iota(jnp.int32, (holders, holders), 1)
    earlier = jnp.where(cols < rows, 1.0, 0.0).astype(BF16)
    first = jnp.dot(earlier, counts, preferred_element_type=F32).astype(jnp.int32)
    offsets = jnp.sum(jnp.where(rows == cols, first, 0), axis=0, keepdims=True)
    offsets_out[...] = jnp.broadcast_to(offsets, offsets_out.shape)
    start = below.astype(jnp.int32)
    window = jnp.concatenate([table, jnp.full((holders, 128), beyond, jnp.int32)], axis=1)
    shift = total // 2
    while shift >= 128:
        keep = shift + 128
        taken = (start & shift) != 0
        taken = jnp.concatenate([taken] * (keep // 128), axis=1)
        window = jnp.where(taken, window[:, shift:shift + keep], window[:, :keep])
        shift //= 2
    while shift >= 1:
        taken = (start & shift) != 0
        taken = jnp.concatenate([taken, taken], axis=1)
        window = jnp.where(taken, pltpu.roll(window, 256 - shift, 1), window)
        shift //= 2
    column = lax.broadcasted_iota(jnp.int32, (holders, width), 1)
    place = jnp.zeros((holders, width), jnp.int32)
    for slot in range(capacity):
        here = window[:, slot:slot + 1] == column
        place = place + jnp.where(here, first[:, :1] + slot, 0)
    place = jnp.sum(place, axis=0, keepdims=True)
    place_out[...] = jnp.broadcast_to(place, place_out.shape)


def arrange_kernel(place, *refs):
    blocks, outs = refs[:len(refs) // 2], refs[len(refs) // 2:]
    width = place.shape[1]
    chunk = 256
    where_to = place[0:1, :]
    for step in range(width // chunk):
        wanted = lax.broadcasted_iota(jnp.int32, (chunk, width), 0) + step * chunk
        pick = jnp.where(wanted == where_to, 1.0, 0.0).astype(BF16)
        for block, out in zip(blocks, outs):
            out[pl.ds(step * chunk, chunk), :] = jnp.dot(
                pick, block[...], preferred_element_type=F32
            ).astype(BF16)


def multiply_kernel(
    offsets, received, amps0, amps1, amps2, amps3, given, left_kept, rows_ref, left
):
    group, core = lax.axis_index("ij"), lax.rem(lax.axis_index("cd"), 2)
    holders, capacity, pairs = received.shape
    width = amps0.shape[0]
    new = lax.broadcasted_iota(jnp.int32, (pairs, pairs), 0)
    old = lax.broadcasted_iota(jnp.int32, (pairs, pairs), 1)
    half = pairs // 2
    chips = half // 2
    side = jnp.where(new < half, core, 1 - core)
    in_half = jnp.where(new < half, new, new - half)
    row = jnp.where(in_half < chips, 0, 1)
    chip = jnp.where(in_half < chips, in_half, in_half - chips)
    pick = jnp.where(old == 4 * chip + 2 * side + row, 1.0, 0.0).astype(BF16)
    chunk = 256
    done = 0
    line = lax.broadcasted_iota(jnp.int32, (8, pairs), 0)
    blank = jnp.zeros((8, pairs), F32)
    for holder in range(holders):
        start = offsets[0, holder]
        aligned = pl.multiple_of((start >> 3) << 3, 8)
        window = jnp.concatenate([received[holder].astype(F32), blank], axis=0)
        window = pltpu.roll(window, start & 7, 0)
        pltpu.store(rows_ref.at[pl.ds(aligned, 8)], window[:8], mask=line >= (start & 7))
        rows_ref[pl.ds(aligned + 8, capacity), :] = window[8:]
        while done + chunk <= width - capacity * (holders - 1 - holder):
            left[:, done:done + chunk] = lax.dot_general(
                pick,
                rows_ref[pl.ds(done, chunk), :].astype(BF16),
                NT,
                preferred_element_type=F32,
            ).astype(BF16)
            done += chunk
    left_kept[...] = left[:half, :]
    cut_product(group, left[half:, :], (amps0, amps1, amps2, amps3), given)


def cut_product(group, left, blocks, target):
    chips = left.shape[0] // 2
    for step, amps in enumerate(blocks):
        block = lax.rem(group + step, 4)
        product = jnp.dot(left, amps[...], preferred_element_type=F32)
        for r in range(2):
            for h in range(2):
                target[pl.ds(r * 8 + 2 * block + h, chips, stride=16), :] = product[
                    r * chips:(r + 1) * chips, h * 128:(h + 1) * 128
                ]


def keep_kernel(left, amps0, amps1, amps2, amps3, kept):
    cut_product(lax.axis_index("ij"), left[...], (amps0, amps1, amps2, amps3), kept)


def pack(owned_columns, ladder_ints, devices, capacity, width):
    pairs, total = ladder_ints.shape
    return pl.pallas_call(
        lambda *refs: pack_kernel(width, *refs),
        out_shape=jax.ShapeDtypeStruct((devices, capacity, pairs), BF16),
        in_specs=[HBM, HBM],
        out_specs=HBM,
        scratch_shapes=[
            pltpu.VMEM((8, total), jnp.int32),
            pltpu.VMEM((pairs, total), BF16),
            pltpu.VMEM((total + capacity + 8, pairs), F32),
            pltpu.VMEM((8, 128), jnp.int32),
            pltpu.SMEM((8, 128), jnp.int32),
            pltpu.VMEM((devices, capacity, pairs), BF16),
            pltpu.SemaphoreType.DMA((11,)),
        ],
        compiler_params=pltpu.CompilerParams(vmem_limit_bytes=VMEM_LIMIT),
        name="pack",
    )(in_hbm(owned_columns), in_hbm(ladder_ints))


def order(owned_columns, capacity, width):
    holders, _ = owned_columns.shape
    return pl.pallas_call(
        lambda *refs: order_kernel(capacity, width, *refs),
        out_shape=[
            jax.ShapeDtypeStruct((8, width), jnp.int32),
            jax.ShapeDtypeStruct((8, holders), jnp.int32),
        ],
        in_specs=[HBM],
        out_specs=[VMEM, VMEM],
        scratch_shapes=[
            pltpu.VMEM(owned_columns.shape, jnp.int32),
            pltpu.SemaphoreType.DMA,
        ],
        compiler_params=pltpu.CompilerParams(vmem_limit_bytes=VMEM_LIMIT),
        name="order",
        cost_estimate=pl.CostEstimate(
            flops=15_000_000_000, bytes_accessed=1_000_000, transcendentals=0
        ),
    )(in_hbm(owned_columns))


def arrange(place, *blocks):
    return pl.pallas_call(
        arrange_kernel,
        out_shape=[jax.ShapeDtypeStruct(block.shape, block.dtype) for block in blocks],
        in_specs=[VMEM] * (1 + len(blocks)),
        out_specs=[VMEM] * len(blocks),
        compiler_params=pltpu.CompilerParams(vmem_limit_bytes=VMEM_LIMIT),
        name="arrange",
        cost_estimate=pl.CostEstimate(
            flops=2_000_000_000, bytes_accessed=2_000_000, transcendentals=0
        ),
    )(place, *blocks)


def multiply(offsets, received, *amps):
    _, capacity, pairs = received.shape
    width, pairs_ij = amps[0].shape
    return pl.pallas_call(
        multiply_kernel,
        out_shape=[
            jax.ShapeDtypeStruct((pairs // 2 * 4 * pairs_ij // 128, 128), F32),
            jax.ShapeDtypeStruct((pairs // 2, width), BF16),
        ],
        in_specs=[SMEM] + [VMEM] * 5,
        out_specs=[VMEM, VMEM],
        scratch_shapes=[
            pltpu.VMEM((width + capacity + 8, pairs), F32),
            pltpu.VMEM((pairs, width), BF16),
        ],
        compiler_params=pltpu.CompilerParams(vmem_limit_bytes=VMEM_LIMIT),
        name="multiply",
    )(offsets, received, *amps)


def keep(left, *amps):
    half, _ = left.shape
    _, pairs_ij = amps[0].shape
    return pl.pallas_call(
        keep_kernel,
        out_shape=jax.ShapeDtypeStruct((half * 4 * pairs_ij // 128, 128), F32),
        in_specs=[VMEM] * 5,
        out_specs=VMEM,
        compiler_params=pltpu.CompilerParams(vmem_limit_bytes=VMEM_LIMIT),
        name="keep",
        cost_estimate=pl.CostEstimate(
            flops=1_000_000_000, bytes_accessed=3_000_000, transcendentals=0
        ),
    )(left, *amps)


SCALE = 2.0 ** 22


def squeeze(value):
    return (jnp.sign(value) * jnp.sqrt(jnp.abs(value) * SCALE)).astype(jnp.float16)


def unsqueeze(root):
    root = root.astype(F32)
    return root * jnp.abs(root) * (1.0 / SCALE)


def body(amplitudes, owned_columns, ladder_ints):
    devices_cd = lax.axis_size("cd")
    groups = lax.axis_size("ij")
    width = amplitudes.shape[0]
    capacity = 2 * width // devices_cd

    outgoing = pack(owned_columns, ladder_ints, devices_cd, capacity, width)
    incoming = lax.all_to_all(outgoing, "cd", split_axis=0, concat_axis=0, tiled=True)
    def from_group(value, step):
        return lax.ppermute(value, "ij", [((i + step) % groups, i) for i in range(groups)])

    amps2 = from_group(amplitudes, 2)
    place, offsets = order(owned_columns, capacity, width)
    later, amps2 = lax.optimization_barrier((amplitudes, amps2))
    amps1, amps3 = from_group(later, 1), from_group(later, 3)
    amps0, amps2 = arrange(place, amplitudes, amps2)
    amps1, amps3 = arrange(place, amps1, amps3)
    given, left = multiply(offsets, incoming, amps0, amps1, amps2, amps3)
    kept = keep(left, amps0, amps1, amps2, amps3)
    taken = lax.ppermute(given, "cd", [(i, i ^ 1) for i in range(devices_cd)])
    both = squeeze(kept + taken).reshape(devices_cd // 2, 16, 128)
    same_core = [[2 * k + c for k in range(devices_cd // 2)] for c in range(2)]
    shares = lax.all_to_all(both, "cd", 0, 0, tiled=True, axis_index_groups=same_core)
    summed = jnp.sum(unsqueeze(shares), axis=0)
    return summed.astype(BF16).reshape(2, 1024)


def solution(mesh):
    return jax.shard_map(
        body,
        mesh=mesh,
        in_specs=(P("cd", "ij"), P(), P("ij", "cd")),
        out_specs=P(("ij", "cd"), None),
        check_vma=False,
    )
```

```python
import jax
import jax.numpy as jnp
from jax import lax
from jax.experimental import pallas as pl
from jax.experimental.pallas import tpu as pltpu
from jax.sharding import PartitionSpec as P

F32 = jnp.float32
BF16 = jnp.bfloat16
NT = (((1,), (1,)), ((), ()))
VMEM_LIMIT = 24 * 1024 * 1024
VMEM = pl.BlockSpec(memory_space=pltpu.VMEM)
SMEM = pl.BlockSpec(memory_space=pltpu.SMEM)
ANY = pl.BlockSpec(memory_space=pl.ANY)
HBM = pl.BlockSpec(memory_space=pltpu.HBM)


def in_hbm(value):
    return pltpu.with_memory_space_constraint(value, pltpu.HBM)


def pack_kernel(width, owned, ints, out, group, staged, slots, firsts, starts, windows, sems):
    device = lax.axis_index("cd")
    devices, capacity, _ = out.shape
    total, chunk = ints.shape[1], 256
    eight = pl.multiple_of((device >> 3) << 3, 8)
    own_copy = pltpu.make_async_copy(owned.at[pl.ds(eight, 8)], group, sems.at[0])
    own_copy.start()
    quarter = total // 4
    ints_copies = []
    for part in range(4):
        at = pl.ds(part * quarter, quarter)
        ints_copies.append(pltpu.make_async_copy(ints.at[:, at], staged.at[:, at], sems.at[11 + part]))
        ints_copies[-1].start()
    slots[pl.ds(total, capacity + 8), :] = jnp.zeros((capacity + 8, slots.shape[1]), F32)
    rows = lax.broadcasted_iota(jnp.int32, (chunk, chunk), 0)
    cols = lax.broadcasted_iota(jnp.int32, (chunk, chunk), 1)
    eye = jnp.where(rows == cols, 1.0, 0.0).astype(BF16)
    line = lax.broadcasted_iota(jnp.int32, group.shape, 0)
    below = lax.broadcasted_iota(jnp.int32, (devices, 128), 0) * width
    same = lax.broadcasted_iota(jnp.int32, (devices, 128), 0) == lax.broadcasted_iota(
        jnp.int32, (devices, 128), 1
    )
    own_copy.wait()
    row = jnp.sum(jnp.where(line == device - eight, group[...], 0), axis=0, keepdims=True)
    row = jnp.where(row < 0, jnp.int32(1 << 30), row)
    before = jnp.zeros((devices, 128), F32)
    for tile in range(total // 128):
        before = before + jnp.where(row[:, tile * 128:(tile + 1) * 128] < below, 1.0, 0.0)
    ones = jnp.ones((128, 128), BF16)
    before = jnp.dot(before.astype(BF16), ones, preferred_element_type=F32)
    first = jnp.sum(jnp.where(same, before, 0.0), axis=0, keepdims=True).astype(jnp.int32)
    firsts[...] = jnp.broadcast_to(first, firsts.shape)
    starts_copy = pltpu.make_async_copy(firsts, starts, sems.at[2])
    starts_copy.start()
    for step in range(total // chunk):
        if step * chunk % quarter == 0:
            ints_copies[step * chunk // quarter].wait()
        at = pl.ds(step * chunk, chunk)
        slots[at, :] = lax.dot_general(eye, staged[:, at], NT, preferred_element_type=F32)
    starts_copy.wait()
    pieces = 8
    each = devices // pieces
    copies = []
    for piece in range(pieces):
        for dest in range(piece * each, (piece + 1) * each):
            start = starts[0, dest]
            aligned = pl.multiple_of((start >> 3) << 3, 8)
            window = slots[pl.ds(aligned, capacity + 8), :]
            window = pltpu.roll(window, capacity + 8 - (start & 7), 0)
            windows[dest] = window[:capacity].astype(BF16)
        at = pl.ds(piece * each, each)
        copies.append(pltpu.make_async_copy(windows.at[at], out.at[at], sems.at[3 + piece]))
        copies[-1].start()
    for copy in copies:
        copy.wait()


def order_kernel(capacity, width, owned, place_out, offsets_out, held, sem):
    copy = pltpu.make_async_copy(owned, held, sem)
    copy.start()
    base = lax.axis_index("cd") * width
    holders, total = owned.shape
    beyond = jnp.int32(1 << 30)
    copy.wait()
    table = held[...]
    table = jnp.where(table < 0, beyond, table - base)
    below = jnp.zeros((holders, 128), F32)
    ended = jnp.zeros((holders, 128), F32)
    for tile in range(total // 128):
        part = table[:, tile * 128:(tile + 1) * 128]
        below = below + jnp.where(part < 0, 1.0, 0.0)
        ended = ended + jnp.where(part < width, 1.0, 0.0)
    ones = jnp.ones((128, 128), BF16)
    below = jnp.dot(below.astype(BF16), ones, preferred_element_type=F32)
    ended = jnp.dot(ended.astype(BF16), ones, preferred_element_type=F32)
    counts = (ended - below).astype(BF16)
    rows = lax.broadcasted_iota(jnp.int32, (holders, holders), 0)
    cols = lax.broadcasted_iota(jnp.int32, (holders, holders), 1)
    earlier = jnp.where(cols < rows, 1.0, 0.0).astype(BF16)
    first = jnp.dot(earlier, counts, preferred_element_type=F32).astype(jnp.int32)
    offsets = jnp.sum(jnp.where(rows == cols, first, 0), axis=0, keepdims=True)
    offsets_out[...] = jnp.broadcast_to(offsets, offsets_out.shape)
    start = below.astype(jnp.int32)
    window = jnp.concatenate([table, jnp.full((holders, 128), beyond, jnp.int32)], axis=1)
    shift = total // 2
    while shift >= 128:
        keep = shift + 128
        taken = (start & shift) != 0
        taken = jnp.concatenate([taken] * (keep // 128), axis=1)
        window = jnp.where(taken, window[:, shift:shift + keep], window[:, :keep])
        shift //= 2
    while shift >= 1:
        taken = (start & shift) != 0
        taken = jnp.concatenate([taken, taken], axis=1)
        window = jnp.where(taken, pltpu.roll(window, 256 - shift, 1), window)
        shift //= 2
    column = lax.broadcasted_iota(jnp.int32, (holders, width), 1)
    place = jnp.zeros((holders, width), jnp.int32)
    for slot in range(capacity):
        here = window[:, slot:slot + 1] == column
        place = place + jnp.where(here, first[:, :1] + slot, 0)
    place = jnp.sum(place, axis=0, keepdims=True)
    place_out[...] = jnp.broadcast_to(place, place_out.shape)


def arrange_kernel(place, *refs):
    blocks, outs = refs[:len(refs) // 2], refs[len(refs) // 2:]
    width = place.shape[1]
    chunk = 256
    where_to = place[0:1, :]
    for step in range(width // chunk):
        wanted = lax.broadcasted_iota(jnp.int32, (chunk, width), 0) + step * chunk
        pick = jnp.where(wanted == where_to, 1.0, 0.0).astype(BF16)
        for block, out in zip(blocks, outs):
            out[pl.ds(step * chunk, chunk), :] = jnp.dot(
                pick, block[...], preferred_element_type=F32
            ).astype(BF16)


def multiply_kernel(
    offsets, received, amps0, amps1, amps2, amps3, given, left_kept, rows_ref, left
):
    group, core = lax.axis_index("ij"), lax.rem(lax.axis_index("cd"), 2)
    holders, capacity, pairs = received.shape
    width = amps0.shape[0]
    new = lax.broadcasted_iota(jnp.int32, (pairs, pairs), 0)
    old = lax.broadcasted_iota(jnp.int32, (pairs, pairs), 1)
    half = pairs // 2
    chips = half // 2
    side = jnp.where(new < half, core, 1 - core)
    in_half = jnp.where(new < half, new, new - half)
    row = jnp.where(in_half < chips, 0, 1)
    chip = jnp.where(in_half < chips, in_half, in_half - chips)
    pick = jnp.where(old == 4 * chip + 2 * side + row, 1.0, 0.0).astype(BF16)
    chunk = 256
    done = 0
    line = lax.broadcasted_iota(jnp.int32, (8, pairs), 0)
    blank = jnp.zeros((8, pairs), F32)
    for holder in range(holders):
        start = offsets[0, holder]
        aligned = pl.multiple_of((start >> 3) << 3, 8)
        window = jnp.concatenate([received[holder].astype(F32), blank], axis=0)
        window = pltpu.roll(window, start & 7, 0)
        pltpu.store(rows_ref.at[pl.ds(aligned, 8)], window[:8], mask=line >= (start & 7))
        rows_ref[pl.ds(aligned + 8, capacity), :] = window[8:]
        while done + chunk <= width - capacity * (holders - 1 - holder):
            left[:, done:done + chunk] = lax.dot_general(
                pick,
                rows_ref[pl.ds(done, chunk), :].astype(BF16),
                NT,
                preferred_element_type=F32,
            ).astype(BF16)
            done += chunk
    left_kept[...] = left[:half, :]
    cut_product(group, left[half:, :], (amps0, amps1, amps2, amps3), given)


def cut_product(group, left, blocks, target):
    chips = left.shape[0] // 2
    for step, amps in enumerate(blocks):
        block = lax.rem(group + step, 4)
        product = jnp.dot(left, amps[...], preferred_element_type=F32)
        for r in range(2):
            for h in range(2):
                target[pl.ds(r * 8 + 2 * block + h, chips, stride=16), :] = product[
                    r * chips:(r + 1) * chips, h * 128:(h + 1) * 128
                ]


def keep_kernel(left, amps0, amps1, amps2, amps3, kept):
    cut_product(lax.axis_index("ij"), left[...], (amps0, amps1, amps2, amps3), kept)


def pack(owned_columns, ladder_ints, devices, capacity, width):
    pairs, total = ladder_ints.shape
    return pl.pallas_call(
        lambda *refs: pack_kernel(width, *refs),
        out_shape=jax.ShapeDtypeStruct((devices, capacity, pairs), BF16),
        in_specs=[HBM, HBM],
        out_specs=HBM,
        scratch_shapes=[
            pltpu.VMEM((8, total), jnp.int32),
            pltpu.VMEM((pairs, total), BF16),
            pltpu.VMEM((total + capacity + 8, pairs), F32),
            pltpu.VMEM((8, 128), jnp.int32),
            pltpu.SMEM((8, 128), jnp.int32),
            pltpu.VMEM((devices, capacity, pairs), BF16),
            pltpu.SemaphoreType.DMA((15,)),
        ],
        compiler_params=pltpu.CompilerParams(vmem_limit_bytes=VMEM_LIMIT),
        name="pack",
    )(in_hbm(owned_columns), in_hbm(ladder_ints))


def order(owned_columns, capacity, width):
    holders, _ = owned_columns.shape
    return pl.pallas_call(
        lambda *refs: order_kernel(capacity, width, *refs),
        out_shape=[
            jax.ShapeDtypeStruct((8, width), jnp.int32),
            jax.ShapeDtypeStruct((8, holders), jnp.int32),
        ],
        in_specs=[HBM],
        out_specs=[VMEM, VMEM],
        scratch_shapes=[
            pltpu.VMEM(owned_columns.shape, jnp.int32),
            pltpu.SemaphoreType.DMA,
        ],
        compiler_params=pltpu.CompilerParams(vmem_limit_bytes=VMEM_LIMIT),
        name="order",
        cost_estimate=pl.CostEstimate(
            flops=15_000_000_000, bytes_accessed=1_000_000, transcendentals=0
        ),
    )(in_hbm(owned_columns))


def arrange(place, *blocks):
    return pl.pallas_call(
        arrange_kernel,
        out_shape=[jax.ShapeDtypeStruct(block.shape, block.dtype) for block in blocks],
        in_specs=[VMEM] * (1 + len(blocks)),
        out_specs=[VMEM] * len(blocks),
        compiler_params=pltpu.CompilerParams(vmem_limit_bytes=VMEM_LIMIT),
        name="arrange",
        cost_estimate=pl.CostEstimate(
            flops=2_000_000_000, bytes_accessed=2_000_000, transcendentals=0
        ),
    )(place, *blocks)


def multiply(offsets, received, *amps):
    _, capacity, pairs = received.shape
    width, pairs_ij = amps[0].shape
    return pl.pallas_call(
        multiply_kernel,
        out_shape=[
            jax.ShapeDtypeStruct((pairs // 2 * 4 * pairs_ij // 128, 128), F32),
            jax.ShapeDtypeStruct((pairs // 2, width), BF16),
        ],
        in_specs=[SMEM] + [VMEM] * 5,
        out_specs=[VMEM, VMEM],
        scratch_shapes=[
            pltpu.VMEM((width + capacity + 8, pairs), F32),
            pltpu.VMEM((pairs, width), BF16),
        ],
        compiler_params=pltpu.CompilerParams(vmem_limit_bytes=VMEM_LIMIT),
        name="multiply",
    )(offsets, received, *amps)


def keep(left, *amps):
    half, _ = left.shape
    _, pairs_ij = amps[0].shape
    return pl.pallas_call(
        keep_kernel,
        out_shape=jax.ShapeDtypeStruct((half * 4 * pairs_ij // 128, 128), F32),
        in_specs=[VMEM] * 5,
        out_specs=VMEM,
        compiler_params=pltpu.CompilerParams(vmem_limit_bytes=VMEM_LIMIT),
        name="keep",
        cost_estimate=pl.CostEstimate(
            flops=1_000_000_000, bytes_accessed=3_000_000, transcendentals=0
        ),
    )(left, *amps)


SCALE = 2.0 ** 22


def squeeze(value):
    return (jnp.sign(value) * jnp.sqrt(jnp.abs(value) * SCALE)).astype(jnp.float16)


def unsqueeze(root):
    root = root.astype(F32)
    return root * jnp.abs(root) * (1.0 / SCALE)


def body(amplitudes, owned_columns, ladder_ints):
    devices_cd = lax.axis_size("cd")
    groups = lax.axis_size("ij")
    width = amplitudes.shape[0]
    capacity = 2 * width // devices_cd

    outgoing = pack(owned_columns, ladder_ints, devices_cd, capacity, width)
    incoming = lax.all_to_all(outgoing, "cd", split_axis=0, concat_axis=0, tiled=True)
    def from_group(value, step):
        return lax.ppermute(value, "ij", [((i + step) % groups, i) for i in range(groups)])

    amps2 = from_group(amplitudes, 2)
    place, offsets = order(owned_columns, capacity, width)
    later, amps2 = lax.optimization_barrier((amplitudes, amps2))
    amps1, amps3 = from_group(later, 1), from_group(later, 3)
    amps0, amps2 = arrange(place, amplitudes, amps2)
    amps1, amps3 = arrange(place, amps1, amps3)
    given, left = multiply(offsets, incoming, amps0, amps1, amps2, amps3)
    kept = keep(left, amps0, amps1, amps2, amps3)
    taken = lax.ppermute(squeeze(given), "cd", [(i, i ^ 1) for i in range(devices_cd)])
    both = squeeze(kept + unsqueeze(taken)).reshape(devices_cd // 2, 16, 128)
    same_core = [[2 * k + c for k in range(devices_cd // 2)] for c in range(2)]
    shares = lax.all_to_all(both, "cd", 0, 0, tiled=True, axis_index_groups=same_core)
    summed = jnp.sum(unsqueeze(shares), axis=0)
    return summed.astype(BF16).reshape(2, 1024)


def solution(mesh):
    return jax.shard_map(
        body,
        mesh=mesh,
        in_specs=(P("cd", "ij"), P(), P("ij", "cd")),
        out_specs=P(("ij", "cd"), None),
        check_vma=False,
    )
```

```python
import jax
import jax.numpy as jnp
from jax import lax
from jax.experimental import pallas as pl
from jax.experimental.pallas import tpu as pltpu
from jax.sharding import PartitionSpec as P

F32 = jnp.float32
BF16 = jnp.bfloat16
NT = (((1,), (1,)), ((), ()))
VMEM_LIMIT = 24 * 1024 * 1024
VMEM = pl.BlockSpec(memory_space=pltpu.VMEM)
SMEM = pl.BlockSpec(memory_space=pltpu.SMEM)
ANY = pl.BlockSpec(memory_space=pl.ANY)
HBM = pl.BlockSpec(memory_space=pltpu.HBM)


def in_hbm(value):
    return pltpu.with_memory_space_constraint(value, pltpu.HBM)


def pack_kernel(width, owned, ints, out, group, staged, slots, firsts, starts, windows, sems):
    device = lax.axis_index("cd")
    devices, capacity, _ = out.shape
    total, chunk = ints.shape[1], 256
    eight = pl.multiple_of((device >> 3) << 3, 8)
    own_copy = pltpu.make_async_copy(owned.at[pl.ds(eight, 8)], group, sems.at[0])
    own_copy.start()
    ints_copy = pltpu.make_async_copy(ints, staged, sems.at[1])
    ints_copy.start()
    slots[pl.ds(total, capacity + 8), :] = jnp.zeros((capacity + 8, slots.shape[1]), F32)
    rows = lax.broadcasted_iota(jnp.int32, (chunk, chunk), 0)
    cols = lax.broadcasted_iota(jnp.int32, (chunk, chunk), 1)
    eye = jnp.where(rows == cols, 1.0, 0.0).astype(BF16)
    line = lax.broadcasted_iota(jnp.int32, group.shape, 0)
    below = lax.broadcasted_iota(jnp.int32, (devices, 128), 0) * width
    same = lax.broadcasted_iota(jnp.int32, (devices, 128), 0) == lax.broadcasted_iota(
        jnp.int32, (devices, 128), 1
    )
    own_copy.wait()
    row = jnp.sum(jnp.where(line == device - eight, group[...], 0), axis=0, keepdims=True)
    row = jnp.where(row < 0, jnp.int32(1 << 30), row)
    before = jnp.zeros((devices, 128), F32)
    for tile in range(total // 128):
        before = before + jnp.where(row[:, tile * 128:(tile + 1) * 128] < below, 1.0, 0.0)
    ones = jnp.ones((128, 128), BF16)
    before = jnp.dot(before.astype(BF16), ones, preferred_element_type=F32)
    first = jnp.sum(jnp.where(same, before, 0.0), axis=0, keepdims=True).astype(jnp.int32)
    firsts[...] = jnp.broadcast_to(first, firsts.shape)
    starts_copy = pltpu.make_async_copy(firsts, starts, sems.at[2])
    starts_copy.start()
    ints_copy.wait()
    for step in range(total // chunk):
        at = pl.ds(step * chunk, chunk)
        slots[at, :] = lax.dot_general(eye, staged[:, at], NT, preferred_element_type=F32)
    starts_copy.wait()
    pieces = sems.shape[0] - 3
    each = devices // pieces
    copies = []
    for piece in range(pieces):
        for dest in range(piece * each, (piece + 1) * each):
            start = starts[0, dest]
            aligned = pl.multiple_of((start >> 3) << 3, 8)
            window = slots[pl.ds(aligned, capacity + 8), :]
            window = pltpu.roll(window, capacity + 8 - (start & 7), 0)
            windows[dest] = window[:capacity].astype(BF16)
        at = pl.ds(piece * each, each)
        copies.append(pltpu.make_async_copy(windows.at[at], out.at[at], sems.at[3 + piece]))
        copies[-1].start()
    for copy in copies:
        copy.wait()


def order_kernel(capacity, width, owned, place_out, offsets_out, held, sem):
    copy = pltpu.make_async_copy(owned, held, sem)
    copy.start()
    base = lax.axis_index("cd") * width
    holders, total = owned.shape
    beyond = jnp.int32(1 << 30)
    copy.wait()
    table = held[...]
    table = jnp.where(table < 0, beyond, table - base)
    below = jnp.zeros((holders, 128), F32)
    ended = jnp.zeros((holders, 128), F32)
    for tile in range(total // 128):
        part = table[:, tile * 128:(tile + 1) * 128]
        below = below + jnp.where(part < 0, 1.0, 0.0)
        ended = ended + jnp.where(part < width, 1.0, 0.0)
    ones = jnp.ones((128, 128), BF16)
    below = jnp.dot(below.astype(BF16), ones, preferred_element_type=F32)
    ended = jnp.dot(ended.astype(BF16), ones, preferred_element_type=F32)
    counts = (ended - below).astype(BF16)
    rows = lax.broadcasted_iota(jnp.int32, (holders, holders), 0)
    cols = lax.broadcasted_iota(jnp.int32, (holders, holders), 1)
    earlier = jnp.where(cols < rows, 1.0, 0.0).astype(BF16)
    first = jnp.dot(earlier, counts, preferred_element_type=F32).astype(jnp.int32)
    offsets = jnp.sum(jnp.where(rows == cols, first, 0), axis=0, keepdims=True)
    offsets_out[...] = jnp.broadcast_to(offsets, offsets_out.shape)
    start = below.astype(jnp.int32)
    window = jnp.concatenate([table, jnp.full((holders, 128), beyond, jnp.int32)], axis=1)
    shift = total // 2
    while shift >= 128:
        keep = shift + 128
        taken = (start & shift) != 0
        taken = jnp.concatenate([taken] * (keep // 128), axis=1)
        window = jnp.where(taken, window[:, shift:shift + keep], window[:, :keep])
        shift //= 2
    while shift >= 1:
        taken = (start & shift) != 0
        taken = jnp.concatenate([taken, taken], axis=1)
        window = jnp.where(taken, pltpu.roll(window, 256 - shift, 1), window)
        shift //= 2
    column = lax.broadcasted_iota(jnp.int32, (holders, width), 1)
    place = jnp.zeros((holders, width), jnp.int32)
    for slot in range(capacity):
        here = window[:, slot:slot + 1] == column
        place = place + jnp.where(here, first[:, :1] + slot, 0)
    place = jnp.sum(place, axis=0, keepdims=True)
    place_out[...] = jnp.broadcast_to(place, place_out.shape)


def arrange_kernel(place, *refs):
    blocks, outs = refs[:len(refs) // 2], refs[len(refs) // 2:]
    width = place.shape[1]
    chunk = 256
    where_to = place[0:1, :]
    for step in range(width // chunk):
        wanted = lax.broadcasted_iota(jnp.int32, (chunk, width), 0) + step * chunk
        pick = jnp.where(wanted == where_to, 1.0, 0.0).astype(BF16)
        for block, out in zip(blocks, outs):
            out[pl.ds(step * chunk, chunk), :] = jnp.dot(
                pick, block[...], preferred_element_type=F32
            ).astype(BF16)


def multiply_kernel(
    offsets, received, amps0, amps1, amps2, amps3, given, left_kept, rows_ref, left
):
    group, core = lax.axis_index("ij"), lax.rem(lax.axis_index("cd"), 2)
    holders, capacity, pairs = received.shape
    width = amps0.shape[0]
    new = lax.broadcasted_iota(jnp.int32, (pairs, pairs), 0)
    old = lax.broadcasted_iota(jnp.int32, (pairs, pairs), 1)
    half = pairs // 2
    chips = half // 2
    side = jnp.where(new < half, core, 1 - core)
    in_half = jnp.where(new < half, new, new - half)
    row = jnp.where(in_half < chips, 0, 1)
    chip = jnp.where(in_half < chips, in_half, in_half - chips)
    pick = jnp.where(old == 4 * chip + 2 * side + row, 1.0, 0.0).astype(BF16)
    chunk = 256
    done = 0
    line = lax.broadcasted_iota(jnp.int32, (8, pairs), 0)
    blank = jnp.zeros((8, pairs), F32)
    for holder in range(holders):
        start = offsets[0, holder]
        aligned = pl.multiple_of((start >> 3) << 3, 8)
        window = jnp.concatenate([received[holder].astype(F32), blank], axis=0)
        window = pltpu.roll(window, start & 7, 0)
        pltpu.store(rows_ref.at[pl.ds(aligned, 8)], window[:8], mask=line >= (start & 7))
        rows_ref[pl.ds(aligned + 8, capacity), :] = window[8:]
        while done + chunk <= width - capacity * (holders - 1 - holder):
            left[:, done:done + chunk] = lax.dot_general(
                pick,
                rows_ref[pl.ds(done, chunk), :].astype(BF16),
                NT,
                preferred_element_type=F32,
            ).astype(BF16)
            done += chunk
    left_kept[...] = left[:half, :]
    cut_product(group, left[half:, :], (amps0, amps1, amps2, amps3), given)


def cut_product(group, left, blocks, target):
    chips = left.shape[0] // 2
    for step, amps in enumerate(blocks):
        block = lax.rem(group + step, 4)
        product = jnp.dot(left, amps[...], preferred_element_type=F32)
        for r in range(2):
            for h in range(2):
                target[pl.ds(r * 8 + 2 * block + h, chips, stride=16), :] = product[
                    r * chips:(r + 1) * chips, h * 128:(h + 1) * 128
                ]


def keep_kernel(left, amps0, amps1, amps2, amps3, kept):
    cut_product(lax.axis_index("ij"), left[...], (amps0, amps1, amps2, amps3), kept)


def pack(owned_columns, ladder_ints, devices, capacity, width):
    pairs, total = ladder_ints.shape
    return pl.pallas_call(
        lambda *refs: pack_kernel(width, *refs),
        out_shape=jax.ShapeDtypeStruct((devices, capacity, pairs), BF16),
        in_specs=[HBM, HBM],
        out_specs=HBM,
        scratch_shapes=[
            pltpu.VMEM((8, total), jnp.int32),
            pltpu.VMEM((pairs, total), BF16),
            pltpu.VMEM((total + capacity + 8, pairs), F32),
            pltpu.VMEM((8, 128), jnp.int32),
            pltpu.SMEM((8, 128), jnp.int32),
            pltpu.VMEM((devices, capacity, pairs), BF16),
            pltpu.SemaphoreType.DMA((11,)),
        ],
        compiler_params=pltpu.CompilerParams(vmem_limit_bytes=VMEM_LIMIT),
        name="pack",
    )(in_hbm(owned_columns), in_hbm(ladder_ints))


def order(owned_columns, capacity, width):
    holders, _ = owned_columns.shape
    return pl.pallas_call(
        lambda *refs: order_kernel(capacity, width, *refs),
        out_shape=[
            jax.ShapeDtypeStruct((8, width), jnp.int32),
            jax.ShapeDtypeStruct((8, holders), jnp.int32),
        ],
        in_specs=[HBM],
        out_specs=[VMEM, VMEM],
        scratch_shapes=[
            pltpu.VMEM(owned_columns.shape, jnp.int32),
            pltpu.SemaphoreType.DMA,
        ],
        compiler_params=pltpu.CompilerParams(vmem_limit_bytes=VMEM_LIMIT),
        name="order",
        cost_estimate=pl.CostEstimate(
            flops=15_000_000_000, bytes_accessed=1_000_000, transcendentals=0
        ),
    )(in_hbm(owned_columns))


def arrange(place, *blocks):
    return pl.pallas_call(
        arrange_kernel,
        out_shape=[jax.ShapeDtypeStruct(block.shape, block.dtype) for block in blocks],
        in_specs=[VMEM] * (1 + len(blocks)),
        out_specs=[VMEM] * len(blocks),
        compiler_params=pltpu.CompilerParams(vmem_limit_bytes=VMEM_LIMIT),
        name="arrange",
        cost_estimate=pl.CostEstimate(
            flops=2_000_000_000, bytes_accessed=2_000_000, transcendentals=0
        ),
    )(place, *blocks)


def multiply(offsets, received, *amps):
    _, capacity, pairs = received.shape
    width, pairs_ij = amps[0].shape
    return pl.pallas_call(
        multiply_kernel,
        out_shape=[
            jax.ShapeDtypeStruct((pairs // 2 * 4 * pairs_ij // 128, 128), F32),
            jax.ShapeDtypeStruct((pairs // 2, width), BF16),
        ],
        in_specs=[SMEM] + [VMEM] * 5,
        out_specs=[VMEM, VMEM],
        scratch_shapes=[
            pltpu.VMEM((width + capacity + 8, pairs), F32),
            pltpu.VMEM((pairs, width), BF16),
        ],
        compiler_params=pltpu.CompilerParams(vmem_limit_bytes=VMEM_LIMIT),
        name="multiply",
    )(offsets, received, *amps)


def keep(left, *amps):
    half, _ = left.shape
    _, pairs_ij = amps[0].shape
    return pl.pallas_call(
        keep_kernel,
        out_shape=jax.ShapeDtypeStruct((half * 4 * pairs_ij // 128, 128), F32),
        in_specs=[VMEM] * 5,
        out_specs=VMEM,
        compiler_params=pltpu.CompilerParams(vmem_limit_bytes=VMEM_LIMIT),
        name="keep",
        cost_estimate=pl.CostEstimate(
            flops=1_000_000_000, bytes_accessed=3_000_000, transcendentals=0
        ),
    )(left, *amps)


SCALE = 2.0 ** 22


def squeeze(value):
    return (jnp.sign(value) * jnp.sqrt(jnp.abs(value) * SCALE)).astype(jnp.float16)


def unsqueeze(root):
    root = root.astype(F32)
    return root * jnp.abs(root) * (1.0 / SCALE)


def body(amplitudes, owned_columns, ladder_ints):
    devices_cd = lax.axis_size("cd")
    groups = lax.axis_size("ij")
    width = amplitudes.shape[0]
    capacity = 2 * width // devices_cd

    outgoing = pack(owned_columns, ladder_ints, devices_cd, capacity, width)
    incoming = lax.all_to_all(outgoing, "cd", split_axis=0, concat_axis=0, tiled=True)
    def from_group(value, step):
        return lax.ppermute(value, "ij", [((i + step) % groups, i) for i in range(groups)])

    amps2 = from_group(amplitudes, 2)
    place, offsets = order(owned_columns, capacity, width)
    later, amps2 = lax.optimization_barrier((amplitudes, amps2))
    amps1, amps3 = from_group(later, 1), from_group(later, 3)
    amps0, amps2 = arrange(place, amplitudes, amps2)
    amps1, amps3 = arrange(place, amps1, amps3)
    given, left = multiply(offsets, incoming, amps0, amps1, amps2, amps3)
    kept = keep(left, amps0, amps1, amps2, amps3)
    taken = lax.ppermute(squeeze(given), "cd", [(i, i ^ 1) for i in range(devices_cd)])
    both = squeeze(kept + unsqueeze(taken)).reshape(devices_cd // 2, 16, 128)
    same_core = [[2 * k + c for k in range(devices_cd // 2)] for c in range(2)]
    shares = lax.all_to_all(both, "cd", 0, 0, tiled=True, axis_index_groups=same_core)
    summed = jnp.sum(unsqueeze(shares), axis=0)
    return summed.astype(BF16).reshape(2, 1024)


def solution(mesh):
    return jax.shard_map(
        body,
        mesh=mesh,
        in_specs=(P("cd", "ij"), P(), P("ij", "cd")),
        out_specs=P(("ij", "cd"), None),
        check_vma=False,
    )
```

```python
import jax
import jax.numpy as jnp
from jax import lax
from jax.experimental import pallas as pl
from jax.experimental.pallas import tpu as pltpu
from jax.sharding import PartitionSpec as P

F32 = jnp.float32
BF16 = jnp.bfloat16
NT = (((1,), (1,)), ((), ()))
VMEM_LIMIT = 24 * 1024 * 1024
VMEM = pl.BlockSpec(memory_space=pltpu.VMEM)
SMEM = pl.BlockSpec(memory_space=pltpu.SMEM)
ANY = pl.BlockSpec(memory_space=pl.ANY)
HBM = pl.BlockSpec(memory_space=pltpu.HBM)


def in_hbm(value):
    return pltpu.with_memory_space_constraint(value, pltpu.HBM)


def pack_kernel(width, owned, ints, out, group, staged, slots, firsts, starts, windows, sems):
    device = lax.axis_index("cd")
    devices, capacity, _ = out.shape
    total, chunk = ints.shape[1], 256
    eight = pl.multiple_of((device >> 3) << 3, 8)
    own_copy = pltpu.make_async_copy(owned.at[pl.ds(eight, 8)], group, sems.at[0])
    own_copy.start()
    ints_copy = pltpu.make_async_copy(ints, staged, sems.at[1])
    ints_copy.start()
    slots[pl.ds(total, capacity + 8), :] = jnp.zeros((capacity + 8, slots.shape[1]), F32)
    rows = lax.broadcasted_iota(jnp.int32, (chunk, chunk), 0)
    cols = lax.broadcasted_iota(jnp.int32, (chunk, chunk), 1)
    eye = jnp.where(rows == cols, 1.0, 0.0).astype(BF16)
    line = lax.broadcasted_iota(jnp.int32, group.shape, 0)
    below = lax.broadcasted_iota(jnp.int32, (devices, 128), 0) * width
    same = lax.broadcasted_iota(jnp.int32, (devices, 128), 0) == lax.broadcasted_iota(
        jnp.int32, (devices, 128), 1
    )
    own_copy.wait()
    row = jnp.sum(jnp.where(line == device - eight, group[...], 0), axis=0, keepdims=True)
    row = jnp.where(row < 0, jnp.int32(1 << 30), row)
    before = jnp.zeros((devices, 128), F32)
    for tile in range(total // 128):
        before = before + jnp.where(row[:, tile * 128:(tile + 1) * 128] < below, 1.0, 0.0)
    ones = jnp.ones((128, 128), BF16)
    before = jnp.dot(before.astype(BF16), ones, preferred_element_type=F32)
    first = jnp.sum(jnp.where(same, before, 0.0), axis=0, keepdims=True).astype(jnp.int32)
    firsts[...] = jnp.broadcast_to(first, firsts.shape)
    starts_copy = pltpu.make_async_copy(firsts, starts, sems.at[2])
    starts_copy.start()
    ints_copy.wait()
    for step in range(total // chunk):
        at = pl.ds(step * chunk, chunk)
        slots[at, :] = lax.dot_general(eye, staged[:, at], NT, preferred_element_type=F32)
    starts_copy.wait()
    pieces = sems.shape[0] - 3
    each = devices // pieces
    copies = []
    for piece in range(pieces):
        for dest in range(piece * each, (piece + 1) * each):
            start = starts[0, dest]
            aligned = pl.multiple_of((start >> 3) << 3, 8)
            window = slots[pl.ds(aligned, capacity + 8), :]
            window = pltpu.roll(window, capacity + 8 - (start & 7), 0)
            windows[dest] = window[:capacity].astype(BF16)
        at = pl.ds(piece * each, each)
        copies.append(pltpu.make_async_copy(windows.at[at], out.at[at], sems.at[3 + piece]))
        copies[-1].start()
    for copy in copies:
        copy.wait()


def order_kernel(capacity, width, owned, place_out, offsets_out, held, sem):
    copy = pltpu.make_async_copy(owned, held, sem)
    copy.start()
    base = lax.axis_index("cd") * width
    holders, total = owned.shape
    beyond = jnp.int32(1 << 30)
    copy.wait()
    table = held[...]
    table = jnp.where(table < 0, beyond, table - base)
    below = jnp.zeros((holders, 128), F32)
    ended = jnp.zeros((holders, 128), F32)
    for tile in range(total // 128):
        part = table[:, tile * 128:(tile + 1) * 128]
        below = below + jnp.where(part < 0, 1.0, 0.0)
        ended = ended + jnp.where(part < width, 1.0, 0.0)
    ones = jnp.ones((128, 128), BF16)
    below = jnp.dot(below.astype(BF16), ones, preferred_element_type=F32)
    ended = jnp.dot(ended.astype(BF16), ones, preferred_element_type=F32)
    counts = (ended - below).astype(BF16)
    rows = lax.broadcasted_iota(jnp.int32, (holders, holders), 0)
    cols = lax.broadcasted_iota(jnp.int32, (holders, holders), 1)
    earlier = jnp.where(cols < rows, 1.0, 0.0).astype(BF16)
    first = jnp.dot(earlier, counts, preferred_element_type=F32).astype(jnp.int32)
    offsets = jnp.sum(jnp.where(rows == cols, first, 0), axis=0, keepdims=True)
    offsets_out[...] = jnp.broadcast_to(offsets, offsets_out.shape)
    start = below.astype(jnp.int32)
    window = jnp.concatenate([table, jnp.full((holders, 128), beyond, jnp.int32)], axis=1)
    shift = total // 2
    while shift >= 128:
        keep = shift + 128
        taken = (start & shift) != 0
        taken = jnp.concatenate([taken] * (keep // 128), axis=1)
        window = jnp.where(taken, window[:, shift:shift + keep], window[:, :keep])
        shift //= 2
    while shift >= 1:
        taken = (start & shift) != 0
        taken = jnp.concatenate([taken, taken], axis=1)
        window = jnp.where(taken, pltpu.roll(window, 256 - shift, 1), window)
        shift //= 2
    column = lax.broadcasted_iota(jnp.int32, (holders, width), 1)
    place = jnp.zeros((holders, width), jnp.int32)
    for slot in range(capacity):
        here = window[:, slot:slot + 1] == column
        place = place + jnp.where(here, first[:, :1] + slot, 0)
    place = jnp.sum(place, axis=0, keepdims=True)
    place_out[...] = jnp.broadcast_to(place, place_out.shape)


def arrange_kernel(place, *refs):
    blocks, outs = refs[:len(refs) // 2], refs[len(refs) // 2:]
    width = place.shape[1]
    chunk = 256
    where_to = place[0:1, :]
    for step in range(width // chunk):
        wanted = lax.broadcasted_iota(jnp.int32, (chunk, width), 0) + step * chunk
        pick = jnp.where(wanted == where_to, 1.0, 0.0).astype(BF16)
        for block, out in zip(blocks, outs):
            out[pl.ds(step * chunk, chunk), :] = jnp.dot(
                pick, block[...], preferred_element_type=F32
            ).astype(BF16)


def multiply_kernel(
    offsets, received, amps0, amps1, amps2, amps3, given, left_kept, rows_ref, left
):
    group, core = lax.axis_index("ij"), lax.rem(lax.axis_index("cd"), 2)
    holders, capacity, pairs = received.shape
    width = amps0.shape[0]
    new = lax.broadcasted_iota(jnp.int32, (pairs, pairs), 0)
    old = lax.broadcasted_iota(jnp.int32, (pairs, pairs), 1)
    half = pairs // 2
    chips = half // 2
    side = jnp.where(new < half, core, 1 - core)
    in_half = jnp.where(new < half, new, new - half)
    row = jnp.where(in_half < chips, 0, 1)
    chip = jnp.where(in_half < chips, in_half, in_half - chips)
    pick = jnp.where(old == 4 * chip + 2 * side + row, 1.0, 0.0).astype(BF16)
    chunk = 256
    done = 0
    line = lax.broadcasted_iota(jnp.int32, (8, pairs), 0)
    blank = jnp.zeros((8, pairs), F32)
    for holder in range(holders):
        start = offsets[0, holder]
        aligned = pl.multiple_of((start >> 3) << 3, 8)
        window = jnp.concatenate([received[holder].astype(F32), blank], axis=0)
        window = pltpu.roll(window, start & 7, 0)
        pltpu.store(rows_ref.at[pl.ds(aligned, 8)], window[:8], mask=line >= (start & 7))
        rows_ref[pl.ds(aligned + 8, capacity), :] = window[8:]
        while done + chunk <= width - capacity * (holders - 1 - holder):
            left[:, done:done + chunk] = lax.dot_general(
                pick,
                rows_ref[pl.ds(done, chunk), :].astype(BF16),
                NT,
                preferred_element_type=F32,
            ).astype(BF16)
            done += chunk
    left_kept[...] = left[:half, :]
    cut_product(group, left[half:, :], (amps0, amps1, amps2, amps3), given)


def cut_product(group, left, blocks, target):
    chips = left.shape[0] // 2
    for step, amps in enumerate(blocks):
        block = lax.rem(group + step, 4)
        product = jnp.dot(left, amps[...], preferred_element_type=F32)
        for r in range(2):
            for h in range(2):
                target[pl.ds(r * 8 + 2 * block + h, chips, stride=16), :] = product[
                    r * chips:(r + 1) * chips, h * 128:(h + 1) * 128
                ]


def keep_kernel(left, amps0, amps1, amps2, amps3, kept):
    cut_product(lax.axis_index("ij"), left[...], (amps0, amps1, amps2, amps3), kept)


def pack(owned_columns, ladder_ints, devices, capacity, width):
    pairs, total = ladder_ints.shape
    return pl.pallas_call(
        lambda *refs: pack_kernel(width, *refs),
        out_shape=jax.ShapeDtypeStruct((devices, capacity, pairs), BF16),
        in_specs=[HBM, HBM],
        out_specs=HBM,
        scratch_shapes=[
            pltpu.VMEM((8, total), jnp.int32),
            pltpu.VMEM((pairs, total), BF16),
            pltpu.VMEM((total + capacity + 8, pairs), F32),
            pltpu.VMEM((8, 128), jnp.int32),
            pltpu.SMEM((8, 128), jnp.int32),
            pltpu.VMEM((devices, capacity, pairs), BF16),
            pltpu.SemaphoreType.DMA((19,)),
        ],
        compiler_params=pltpu.CompilerParams(vmem_limit_bytes=VMEM_LIMIT),
        name="pack",
    )(in_hbm(owned_columns), in_hbm(ladder_ints))


def order(owned_columns, capacity, width):
    holders, _ = owned_columns.shape
    return pl.pallas_call(
        lambda *refs: order_kernel(capacity, width, *refs),
        out_shape=[
            jax.ShapeDtypeStruct((8, width), jnp.int32),
            jax.ShapeDtypeStruct((8, holders), jnp.int32),
        ],
        in_specs=[HBM],
        out_specs=[VMEM, VMEM],
        scratch_shapes=[
            pltpu.VMEM(owned_columns.shape, jnp.int32),
            pltpu.SemaphoreType.DMA,
        ],
        compiler_params=pltpu.CompilerParams(vmem_limit_bytes=VMEM_LIMIT),
        name="order",
        cost_estimate=pl.CostEstimate(
            flops=15_000_000_000, bytes_accessed=1_000_000, transcendentals=0
        ),
    )(in_hbm(owned_columns))


def arrange(place, *blocks):
    return pl.pallas_call(
        arrange_kernel,
        out_shape=[jax.ShapeDtypeStruct(block.shape, block.dtype) for block in blocks],
        in_specs=[VMEM] * (1 + len(blocks)),
        out_specs=[VMEM] * len(blocks),
        compiler_params=pltpu.CompilerParams(vmem_limit_bytes=VMEM_LIMIT),
        name="arrange",
        cost_estimate=pl.CostEstimate(
            flops=2_000_000_000, bytes_accessed=2_000_000, transcendentals=0
        ),
    )(place, *blocks)


def multiply(offsets, received, *amps):
    _, capacity, pairs = received.shape
    width, pairs_ij = amps[0].shape
    return pl.pallas_call(
        multiply_kernel,
        out_shape=[
            jax.ShapeDtypeStruct((pairs // 2 * 4 * pairs_ij // 128, 128), F32),
            jax.ShapeDtypeStruct((pairs // 2, width), BF16),
        ],
        in_specs=[SMEM] + [VMEM] * 5,
        out_specs=[VMEM, VMEM],
        scratch_shapes=[
            pltpu.VMEM((width + capacity + 8, pairs), F32),
            pltpu.VMEM((pairs, width), BF16),
        ],
        compiler_params=pltpu.CompilerParams(vmem_limit_bytes=VMEM_LIMIT),
        name="multiply",
    )(offsets, received, *amps)


def keep(left, *amps):
    half, _ = left.shape
    _, pairs_ij = amps[0].shape
    return pl.pallas_call(
        keep_kernel,
        out_shape=jax.ShapeDtypeStruct((half * 4 * pairs_ij // 128, 128), F32),
        in_specs=[VMEM] * 5,
        out_specs=VMEM,
        compiler_params=pltpu.CompilerParams(vmem_limit_bytes=VMEM_LIMIT),
        name="keep",
        cost_estimate=pl.CostEstimate(
            flops=1_000_000_000, bytes_accessed=3_000_000, transcendentals=0
        ),
    )(left, *amps)


SCALE = 2.0 ** 22


def squeeze(value):
    return (jnp.sign(value) * jnp.sqrt(jnp.abs(value) * SCALE)).astype(jnp.float16)


def unsqueeze(root):
    root = root.astype(F32)
    return root * jnp.abs(root) * (1.0 / SCALE)


def body(amplitudes, owned_columns, ladder_ints):
    devices_cd = lax.axis_size("cd")
    groups = lax.axis_size("ij")
    width = amplitudes.shape[0]
    capacity = 2 * width // devices_cd

    outgoing = pack(owned_columns, ladder_ints, devices_cd, capacity, width)
    incoming = lax.all_to_all(outgoing, "cd", split_axis=0, concat_axis=0, tiled=True)
    def from_group(value, step):
        return lax.ppermute(value, "ij", [((i + step) % groups, i) for i in range(groups)])

    amps2 = from_group(amplitudes, 2)
    place, offsets = order(owned_columns, capacity, width)
    later, amps2 = lax.optimization_barrier((amplitudes, amps2))
    amps1, amps3 = from_group(later, 1), from_group(later, 3)
    amps0, amps2 = arrange(place, amplitudes, amps2)
    amps1, amps3 = arrange(place, amps1, amps3)
    given, left = multiply(offsets, incoming, amps0, amps1, amps2, amps3)
    kept = keep(left, amps0, amps1, amps2, amps3)
    taken = lax.ppermute(given, "cd", [(i, i ^ 1) for i in range(devices_cd)])
    both = squeeze(kept + taken).reshape(devices_cd // 2, 16, 128)
    same_core = [[2 * k + c for k in range(devices_cd // 2)] for c in range(2)]
    shares = lax.all_to_all(both, "cd", 0, 0, tiled=True, axis_index_groups=same_core)
    summed = jnp.sum(unsqueeze(shares), axis=0)
    return summed.astype(BF16).reshape(2, 1024)


def solution(mesh):
    return jax.shard_map(
        body,
        mesh=mesh,
        in_specs=(P("cd", "ij"), P(), P("ij", "cd")),
        out_specs=P(("ij", "cd"), None),
        check_vma=False,
    )
```
